256 devices in a mesh: graph: 32 (over z, y), attn: 8 (over x, core).
Axes of the slice: x: 4, y: 4, z: 8, core: 2. Of those that a mesh axis runs over, the one named last changes fastest.
Arguments:
- features: bfloat16 [131072, 1024], P(('graph', 'attn')), may hold values from -6 to 6
- send_rows: int32 [256, 32, 64], P(('graph', 'attn')), may hold values from 0 to 511
- send_count: int32 [256, 32], P(('graph', 'attn')), may hold values from 32 to 64, as said below
- edge_blocks: int32 [1024, 6], P(('graph', 'attn')), may hold values from 0 to 19, as said below
- edge_weight: int32 [1024, 6, 128, 128], P(('graph', 'attn')), may hold values from 0 to 3
- mask_blocks: int32 [32, 32, 16], P('graph'), may hold values from 0 to 31, as said below
- norm_gain: float32 [1024], replicated, may hold values from 0.5 to 1.5
- query_weight: bfloat16 [1024, 1024], replicated, may hold values from -1 to 1
- key_weight: bfloat16 [1024, 1024], replicated, may hold values from -3 to 3
- value_weight: bfloat16 [1024, 1024], replicated, may hold values from -0.1875 to 0.1875
- out_weight: bfloat16 [1024, 1024], replicated, may hold values from -0.1875 to 0.1875
Outputs:
- updated: bfloat16 [131072, 1024], P(('graph', 'attn'))
The draws below stay inside these ranges and needn't reach their ends.
Inputs may be any that keep to these rules, and one draw needn't show every extreme that they name: `send_count`: each device sends at least half of its 64 slots, rounded up, to every partition; at least one partition gets all 64 slots from each device. `edge_blocks`: the 6 numbers of a destination block are distinct and the first is the destination block's own block; numbers below 4 name the device's own blocks, the others its halo blocks in order; every halo block of a device is named by some destination block of that device. `mask_blocks`: the 16 numbers of a query block are distinct and include the query block itself.
All inputs are finite; a program needn't handle non-finite values.
Results may differ from the reference program's by a relative error of at most 0.007.
Values may be sent and summed in bfloat16 or wider, within the bound.
A program may use at most 128 MiB of HBM per device.

```python
import jax
import jax.numpy as jnp
from jax import lax

D = 1024
HEADS = 16
HEAD_DIM = 64
BLOCK = 128
NB = 6
KB = 16
ROWS_DEV = 512
HALO_DEV = 2048
SLOT = 64
LOCAL_BLOCKS = 4
HALO_BLOCKS = 16
QUERY_BLOCKS = 32
NODES = 131072
N_GRAPH = 32
N_ATTN = 8


def draw_send_count(key, part):
    key = jax.random.fold_in(key, 3)
    first_key, third_key = jax.random.split(key, 2)
    senders = N_GRAPH * N_ATTN
    counts = jax.random.randint(first_key, (senders, N_GRAPH), (SLOT + 1) // 2, SLOT + 1)
    filled = jax.random.randint(third_key, (senders, 1), 0, N_GRAPH)
    counts = jnp.where(jnp.arange(N_GRAPH)[None, :] == filled, SLOT, counts)
    return counts.astype(jnp.int32)


def distinct_with(row_key, needed, choices, taken):
    order = jax.random.permutation(row_key, choices)
    leading = order[0]
    order = jnp.where(order == needed, leading, order)
    order = order.at[0].set(needed)
    return order[:taken]


def device_blocks(dev_key):
    shift_key, order_key = jax.random.split(dev_key)
    sources = LOCAL_BLOCKS + HALO_BLOCKS
    shift = jax.random.randint(shift_key, (), 0, LOCAL_BLOCKS)
    source_ids = jnp.arange(sources, dtype=jnp.int32)
    dest_ids = jnp.arange(LOCAL_BLOCKS, dtype=jnp.int32)
    owner = (source_ids - LOCAL_BLOCKS + shift) % LOCAL_BLOCKS
    mandated = (source_ids[None, :] >= LOCAL_BLOCKS) & (owner[None, :] == dest_ids[:, None])
    ranks = jax.vmap(lambda row_key: jax.random.permutation(row_key, sources))(jax.random.split(order_key, LOCAL_BLOCKS))
    score = jnp.where(mandated, 0, 1) * sources + ranks
    score = jnp.where(source_ids[None, :] == dest_ids[:, None], 3 * sources, score)
    order = jnp.argsort(score, axis=1, stable=True)[:, :NB - 1].astype(jnp.int32)
    return jnp.concatenate([dest_ids[:, None], order], axis=1)


def draw_edge_blocks(key, part):
    key = jax.random.fold_in(key, 5)
    devices = NODES // ROWS_DEV
    dev_keys = jax.random.split(key, devices)
    picked = jax.vmap(device_blocks)(dev_keys)
    return picked.reshape(NODES // BLOCK, NB).astype(jnp.int32)


def draw_edge_weight(key, part):
    first_key, second_key = jax.random.split(key)
    shape = (NODES // BLOCK, NB, BLOCK, BLOCK)
    present = jax.random.randint(first_key, shape, 0, 4) == 0
    levels = jax.random.randint(second_key, shape, 1, 4)
    return jnp.where(present, levels, 0).astype(jnp.int32)


def draw_mask_blocks(key, part):
    key = jax.random.fold_in(key, 7)
    row_total = N_GRAPH * QUERY_BLOCKS
    row_keys = jax.random.split(key, row_total)
    needed = jnp.arange(row_total, dtype=jnp.int32) % QUERY_BLOCKS
    picked = jax.vmap(lambda row_key, wanted: distinct_with(row_key, wanted, QUERY_BLOCKS, KB))(row_keys, needed)
    return picked.reshape(N_GRAPH, QUERY_BLOCKS, KB).astype(jnp.int32)


def projection_pair(key):
    base = jax.random.fold_in(key, 11)
    first_key = jax.random.fold_in(base, 0)
    third_key = jax.random.fold_in(base, 2)
    queries = jax.random.normal(first_key, (D, D), jnp.float32) * D ** (-0.5)
    keyed = jax.random.normal(third_key, (D, D), jnp.float32) * D ** (-0.5)
    return (jnp.clip(queries, -1.0, 1.0), jnp.clip(keyed, -3.0, 3.0))


def draw_query_weight(key, part):
    return projection_pair(key)[0].astype(jnp.bfloat16)


def draw_key_weight(key, part):
    return projection_pair(key)[1].astype(jnp.bfloat16)


def touch_ends(entries, key, low, high):
    place = [jax.random.randint(jax.random.fold_in(key, axis), (), 0, length) for axis, length in enumerate(entries.shape)]
    widest = entries.shape.index(max(entries.shape))
    neighbour = place[:widest] + [(place[widest] + 1) % entries.shape[widest]] + place[widest + 1:]
    return entries.at[tuple(place)].set(low).at[tuple(neighbour)].set(high)


def block_scale(stream_key, extent, cuts, least, top_value):
    level = 1.0
    for axis_at, blocks in cuts:
        heights = jax.random.uniform(jax.random.fold_in(jax.random.fold_in(stream_key, 6), axis_at), (blocks,), jnp.float32, least / len(cuts), top_value / len(cuts))
        level = level * jnp.repeat(jnp.exp(heights), extent[axis_at] // blocks).reshape((-1,) + (1,) * (len(extent) - 1 - axis_at))
    return level


def scatter_about(own_key, extent, deviation, bound, cuts=(), kind=jnp.bfloat16):
    values = jax.random.normal(own_key, extent, jnp.float32) * deviation
    if len(cuts) > 0:
        values = block_scale(own_key, extent, cuts, -0.22, 0.18) * values
    return jnp.clip(values, min=-bound, max=bound).astype(kind)


def setup_inputs(seed: int = 0) -> dict:
    key_of = jax.random.split(jax.random.key(seed), 12)
    features = scatter_about(key_of[0], (NODES, D), 1.0, 6.0, ((0, 256),))
    send_rows = touch_ends(jax.random.randint(key_of[1], (N_GRAPH * N_ATTN, N_GRAPH, SLOT), 0, ROWS_DEV), jax.random.fold_in(key_of[1], 1), 0, ROWS_DEV - 1).astype(jnp.int32)
    send_count = draw_send_count(jax.random.fold_in(key_of[11], 71), 0)
    edge_blocks = draw_edge_blocks(jax.random.fold_in(key_of[11], 71), 0)
    edge_weight = draw_edge_weight(jax.random.fold_in(key_of[11], 71), 0)
    mask_blocks = draw_mask_blocks(jax.random.fold_in(key_of[11], 71), 0)
    norm_gain = jnp.clip(1.0 + 0.1 * jax.random.normal(key_of[6], (D,), jnp.float32), 0.5, 1.5)
    query_weight = draw_query_weight(jax.random.fold_in(key_of[11], 71), 0)
    key_weight = draw_key_weight(jax.random.fold_in(key_of[11], 71), 0)
    value_weight = scatter_about(key_of[9], (D, D), D ** -0.5, 0.1875)
    out_weight = scatter_about(key_of[10], (D, D), D ** -0.5, 0.1875)
    return dict(features=features, send_rows=send_rows, send_count=send_count, edge_blocks=edge_blocks, edge_weight=edge_weight, mask_blocks=mask_blocks, norm_gain=norm_gain, query_weight=query_weight, key_weight=key_weight, value_weight=value_weight, out_weight=out_weight)


EPSILON = 1e-06

def aggregate_rows(own_rows, halo, blocks, weights):
    source = jnp.concatenate([own_rows, halo], axis=0).reshape(-1, BLOCK, D)
    picked = jnp.take(source, blocks.reshape(-1), axis=0).reshape(blocks.shape + (BLOCK, D))
    weight_float = weights.astype(jnp.float32)
    summed = jnp.einsum('bnij,bnjd->bid', weight_float, picked.astype(jnp.float32))
    degree = lax.optimization_barrier(jnp.sum(weights, axis=(1, 3))).astype(jnp.float32)
    result = (own_rows.reshape(-1, BLOCK, D).astype(jnp.float32) + summed) * lax.rsqrt(1.0 + degree)[:, :, None]
    return result.reshape(-1, D).astype(jnp.bfloat16)

def partition_attention(query_rows, key_rows, value_rows, mask):
    blocks = query_rows.shape[0] // BLOCK
    key_blocks = key_rows.reshape(blocks, BLOCK, D)
    value_blocks = value_rows.reshape(blocks, BLOCK, D)
    score_scale = HEAD_DIM ** (-0.5)

    def one_block(block_index):
        queries = lax.dynamic_slice_in_dim(query_rows, block_index * BLOCK, BLOCK, 0)
        queries = queries.reshape(BLOCK, HEADS, HEAD_DIM).astype(jnp.float32)
        chosen = mask[block_index]
        keyset = jnp.take(key_blocks, chosen, axis=0).reshape(-1, HEADS, HEAD_DIM).astype(jnp.float32)
        valueset = jnp.take(value_blocks, chosen, axis=0).reshape(-1, HEADS, HEAD_DIM).astype(jnp.float32)
        scores = jnp.einsum('qhd,khd->hqk', queries, keyset) * score_scale
        row_max = lax.optimization_barrier(jnp.max(scores, axis=-1, keepdims=True))
        raised = jnp.exp(scores - row_max)
        probs = (raised / lax.optimization_barrier(jnp.sum(raised, axis=-1, keepdims=True))).astype(jnp.bfloat16)
        mixed = jnp.einsum('hqk,khd->qhd', probs.astype(jnp.float32), valueset)
        return mixed.astype(jnp.bfloat16).reshape(BLOCK, D)
    return lax.map(one_block, jnp.arange(blocks, dtype=jnp.int32)).reshape(-1, D)

def reference(features, send_rows, send_count, edge_blocks, edge_weight, mask_blocks, norm_gain, query_weight, key_weight, value_weight, out_weight):
    devices = N_GRAPH * N_ATTN
    feats = features.reshape(N_GRAPH, N_ATTN, ROWS_DEV, D)
    rows_four = send_rows.reshape(N_GRAPH, N_ATTN, N_GRAPH, SLOT)
    count_three = send_count.reshape(N_GRAPH, N_ATTN, N_GRAPH)
    blocks_three = edge_blocks.reshape(devices, LOCAL_BLOCKS, NB)
    weights_four = edge_weight.reshape(devices, LOCAL_BLOCKS, NB, BLOCK, BLOCK)

    def one_device(device):
        graph_index = device // N_ATTN
        attn_index = device % N_ATTN
        column = jnp.take(feats, attn_index, axis=1)
        indices = jnp.take(jnp.take(rows_four, attn_index, axis=1), graph_index, axis=1)
        counts = jnp.take(jnp.take(count_three, attn_index, axis=1), graph_index, axis=1)
        picked = jax.vmap(lambda table, which: jnp.take(table, which, axis=0))(column, indices)
        living = jnp.arange(SLOT, dtype=jnp.int32)[None, :] < counts[:, None]
        halo = jnp.where(living[:, :, None], picked, jnp.zeros_like(picked)).reshape(HALO_DEV, D)
        own_rows = jnp.take(column, graph_index, axis=0)
        return aggregate_rows(own_rows, halo, blocks_three[device], weights_four[device])
    aggregated = lax.map(one_device, jnp.arange(devices, dtype=jnp.int32)).reshape(NODES, D)
    values = aggregated.astype(jnp.float32)
    normed = (values * lax.rsqrt(lax.optimization_barrier(jnp.mean(values * values, axis=1, keepdims=True)) + EPSILON) * norm_gain.astype(jnp.float32)).astype(jnp.bfloat16)
    query_rows = jnp.dot(normed, query_weight, preferred_element_type=jnp.float32).astype(jnp.bfloat16)
    key_rows = jnp.dot(normed, key_weight, preferred_element_type=jnp.float32).astype(jnp.bfloat16)
    value_rows = jnp.dot(normed, value_weight, preferred_element_type=jnp.float32).astype(jnp.bfloat16)
    shard_rows = ROWS_DEV * N_ATTN

    def one_partition(group_index):
        first_row = group_index * shard_rows
        return partition_attention(lax.dynamic_slice_in_dim(query_rows, first_row, shard_rows, 0), lax.dynamic_slice_in_dim(key_rows, first_row, shard_rows, 0), lax.dynamic_slice_in_dim(value_rows, first_row, shard_rows, 0), mask_blocks[group_index])
    attended = lax.map(one_partition, jnp.arange(N_GRAPH, dtype=jnp.int32)).reshape(NODES, D)
    updated = jnp.dot(attended, out_weight, preferred_element_type=jnp.float32) + values
    return updated.astype(jnp.bfloat16)
```

```python
import jax
import jax.numpy as jnp
from jax import lax
from jax.experimental import pallas as pl
from jax.experimental.pallas import tpu as pltpu
from jax.sharding import PartitionSpec as P

HEAD_DIM = 64
BLOCK = 128


EPSILON = 1e-06


def gather_halo(features, row_lists, live_counts):
    groups, slot_count = row_lists.shape
    row_count = features.shape[0]
    living = jnp.arange(slot_count, dtype=jnp.int32)[None, :] < live_counts[:, None]
    chosen = jnp.where(living, row_lists, -1).reshape(-1)
    pick = (chosen[:, None] == jnp.arange(row_count, dtype=jnp.int32)[None, :]).astype(jnp.bfloat16)
    picked = jnp.dot(pick, features, preferred_element_type=jnp.float32).astype(jnp.bfloat16)
    return picked.reshape(groups, slot_count, features.shape[1])


def finish(features, summed, edge_weight):
    row_count, model_width = features.shape
    degree = jnp.sum(edge_weight, axis=(1, 3)).astype(jnp.float32)
    own_rows = features.reshape(-1, BLOCK, model_width).astype(jnp.float32)
    result = (own_rows + summed) * lax.rsqrt(1.0 + degree)[:, :, None]
    return result.reshape(row_count, model_width).astype(jnp.bfloat16)


def aggregate(features, halo, edge_blocks, edge_weight):
    model_width = features.shape[1]
    source = jnp.concatenate([features, halo], axis=0).reshape(-1, BLOCK, model_width)
    picked = jnp.take(source, edge_blocks.reshape(-1), axis=0).reshape(
        edge_blocks.shape + (BLOCK, model_width)
    )
    weights = edge_weight.astype(jnp.bfloat16)
    summed = jnp.einsum("bnij,bnjd->bid", weights, picked, preferred_element_type=jnp.float32)
    return finish(features, summed, edge_weight)


def normalize(aggregated, norm_gain):
    values = aggregated.astype(jnp.float32)
    scaled = values * lax.rsqrt(jnp.mean(values * values, axis=1, keepdims=True) + EPSILON)
    return (scaled * norm_gain).astype(jnp.bfloat16)


def attend_kernel(mask_ref, joined_ref, out_ref, scores_a, scores_b):
    width = 2 * HEAD_DIM
    blocks, keys = mask_ref.shape
    first = lax.broadcasted_iota(jnp.int32, (BLOCK, width), 1) < HEAD_DIM
    ones = jnp.ones((2 * BLOCK, width), jnp.bfloat16)

    def rows_of(block):
        return pl.ds(pl.multiple_of(block * BLOCK, BLOCK), BLOCK)

    def pair(block, step, column):
        cols = slice(column * width, (column + 1) * width)
        low = joined_ref[rows_of(mask_ref[block, 2 * step]), cols]
        high = joined_ref[rows_of(mask_ref[block, 2 * step + 1]), cols]
        return jnp.concatenate([low, high], axis=0)

    def score(block, scores):
        query = joined_ref[rows_of(block), 0:width] * jnp.bfloat16(HEAD_DIM ** (-0.5))
        zero = jnp.zeros_like(query)
        query = jnp.concatenate(
            [jnp.where(first, query, zero), jnp.where(first, zero, query)], axis=0
        )
        top = None
        for step in range(keys // 2):
            part = lax.dot_general(
                query, pair(block, step, 1), (((1,), (1,)), ((), ())),
                preferred_element_type=jnp.float32,
            )
            scores[:, 2 * step * BLOCK : (2 * step + 2) * BLOCK] = part
            part = jnp.maximum(part[:, :BLOCK], part[:, BLOCK:])
            top = part if top is None else jnp.maximum(top, part)
        return jnp.max(top, axis=1, keepdims=True)

    def mix(block, scores, top):
        total = jnp.zeros((2 * BLOCK, 2 * width), jnp.float32)
        for step in range(keys // 2):
            values = jnp.concatenate([pair(block, step, 2), ones], axis=1)
            part = scores[:, 2 * step * BLOCK : (2 * step + 2) * BLOCK]
            raised = jnp.exp(part - top).astype(jnp.bfloat16)
            total = total + jnp.dot(raised, values, preferred_element_type=jnp.float32)
        result = total[:, :width] / total[:, width:]
        out_ref[rows_of(block), :] = jnp.where(first, result[:BLOCK], result[BLOCK:]).astype(
            jnp.bfloat16
        )

    def two(index, carry):
        top_a = score(2 * index, scores_a)
        top_b = score(2 * index + 1, scores_b)
        mix(2 * index, scores_a, top_a)
        mix(2 * index + 1, scores_b, top_b)
        return carry

    lax.fori_loop(0, blocks // 2, two, 0)


def attend_blocks(joined, mask):
    keys = mask.shape[1] * BLOCK
    return pl.pallas_call(
        attend_kernel,
        out_shape=jax.ShapeDtypeStruct((joined.shape[0], 2 * HEAD_DIM), jnp.bfloat16),
        in_specs=[
            pl.BlockSpec(memory_space=pltpu.SMEM),
            pl.BlockSpec(memory_space=pltpu.VMEM),
        ],
        out_specs=pl.BlockSpec(memory_space=pltpu.VMEM),
        scratch_shapes=[pltpu.VMEM((2 * BLOCK, keys), jnp.float32)] * 2,
        compiler_params=pltpu.CompilerParams(vmem_limit_bytes=40 * 2**20),
    )(mask, joined)


def on_device(
    features,
    send_rows,
    send_count,
    edge_blocks,
    edge_weight,
    mask_blocks,
    norm_gain,
    query_weight,
    key_weight,
    value_weight,
    out_weight,
):
    outgoing = gather_halo(features, send_rows[0], send_count[0])
    model_width = features.shape[1]
    incoming = lax.all_to_all(outgoing, "graph", split_axis=0, concat_axis=0, tiled=True)
    halo = incoming.reshape(-1, model_width)
    aggregated = aggregate(features, halo, edge_blocks, edge_weight)
    normed = normalize(aggregated, norm_gain)
    head_width = query_weight.shape[1] // lax.axis_size("attn")
    first_col = lax.axis_index("attn") * head_width
    own_columns = jnp.concatenate(
        [
            lax.dynamic_slice_in_dim(matrix, first_col, head_width, 1)
            for matrix in (query_weight, key_weight, value_weight)
        ],
        axis=1,
    )
    joined = jnp.dot(
        lax.all_gather(normed, "attn", axis=0, tiled=True),
        own_columns,
        preferred_element_type=jnp.float32,
    ).astype(jnp.bfloat16)
    attended = attend_blocks(joined, mask_blocks[0])
    returned = lax.all_to_all(attended, "attn", split_axis=0, concat_axis=1, tiled=True)
    updated = jnp.dot(returned, out_weight, preferred_element_type=jnp.float32) + aggregated.astype(
        jnp.float32
    )
    return updated.astype(jnp.bfloat16)


def solution(mesh):
    placed = (
        P(("graph", "attn"), None),
        P(("graph", "attn"), None, None),
        P(("graph", "attn"), None),
        P(("graph", "attn"), None),
        P(("graph", "attn"), None, None, None),
        P("graph", None, None),
        P(),
        P(),
        P(),
        P(),
        P(),
    )
    return jax.shard_map(
        on_device, mesh=mesh, in_specs=placed, out_specs=P(("graph", "attn"), None), check_vma=False
    )
```

```python
import jax
import jax.numpy as jnp
from jax import lax
from jax.experimental import pallas as pl
from jax.experimental.pallas import tpu as pltpu
from jax.sharding import PartitionSpec as P

HEAD_DIM = 64
BLOCK = 128
EPSILON = 1e-06
NZ = 8
NY = 4
NX = 4
SLOT = 64
CHUNKS = (256, 256, 256, 256)
AHEAD = 1
PLUS = (0, 1)
MINUS = (2, 3)
f32 = jnp.float32
bf16 = jnp.bfloat16


def spread_kernel(
    features, slots, blocks_ref, edges, gain, query_hbm, key_hbm, value_hbm,
    joined, own_out, *scratch,
):
    count = len(CHUNKS)
    starts = [sum(CHUNKS[:c]) for c in range(count)]
    scratch = list(scratch)
    source = [scratch.pop(0) for _ in range(count)]
    tables = [scratch.pop(0) for _ in range(count)]
    staged = [scratch.pop(0) for _ in range(count)]
    gathered = [scratch.pop(0) for _ in range(count)]
    (
        slots_in, picks, weights, scale, columns, folded, total, squares,
        column_sem, slot_send, slot_recv, table_send, table_recv, halo_send, halo_recv,
        ring_send, ring_recv, pair_send, pair_recv,
    ) = scratch
    rows = features.shape[0]
    own = rows // BLOCK
    graph = lax.axis_index("graph")
    attn = lax.axis_index("attn")
    z, y = graph // NY, graph % NY
    x, core = attn // 2, attn % 2

    def part(dz, dy=0):
        return lax.rem(z + dz + NZ, NZ) * NY + lax.rem(y + dy, NY)

    def peer(dx, flip=0):
        return lax.rem(x + dx + NX, NX) * 2 + (core if flip == 0 else 1 - core)

    def remote(src, dst, send, recv, to):
        return pltpu.make_async_remote_copy(
            src_ref=src, dst_ref=dst, send_sem=send, recv_sem=recv,
            device_id=to, device_id_type=pl.DeviceIdType.MESH,
        )

    width = 2 * HEAD_DIM
    first_col = pl.multiple_of(attn * width, width)
    loads = [
        pltpu.make_async_copy(
            ref.at[:, pl.ds(first_col, width)], columns.at[k], column_sem.at[k]
        )
        for k, ref in enumerate((query_hbm, key_hbm, value_hbm))
    ]
    for load in loads:
        load.start()
    for c in range(count):
        source[c][0:own] = features[:, starts[c] : starts[c] + CHUNKS[c]].reshape(
            own, BLOCK, CHUNKS[c]
        )

    barrier = pltpu.get_barrier_semaphore()
    near = {(0, dy) for dy in range(1, NY)}
    near |= {(dz, dy) for dz in (1, -1) for dy in range(NY)}
    for dy in PLUS:
        near |= {(2, dy), (-2, -dy % NY)}
    for dy in MINUS:
        near |= {(-2, dy), (2, -dy % NY)}
    near = sorted(near)
    greeted = [(part(dz, dy), attn) for dz, dy in near]
    greeted += [(graph, peer(1)), (graph, peer(-1)), (graph, peer(0, 1))]
    for device in greeted:
        pl.semaphore_signal(barrier, inc=1, device_id=device, device_id_type=pl.DeviceIdType.MESH)
    pl.semaphore_wait(barrier, len(greeted))

    def go(copy):
        copy.start()

    ring = [1, -1]

    def slot_copy(k, src):
        return remote(
            src, slots_in.at[k], slot_send.at[k], slot_recv.at[k], (part(ring[k % 2]), attn)
        )

    def table_copy(c, k, src):
        return remote(
            src, tables[c].at[k], table_send.at[c, k], table_recv.at[c, k],
            (part(ring[k % 2]), attn),
        )

    def send_own(c):
        for k in range(2):
            go(table_copy(c, k, source[c].at[0:own]))

    for k in range(2):
        go(slot_copy(k, slots))
    for c in range(AHEAD):
        send_own(c)

    plan = [(0, [(0, dy) for dy in range(NY)])]
    for side in (1, -1):
        plan.append((-side, [(0, dy) for dy in range(NY)]))
    for side, far in ((1, PLUS), (-1, MINUS)):
        plan.append(
            (
                -2 * side,
                [(0, dy) for dy in range(NY)]
                + [(side, dy) for dy in range(NY)]
                + [(2 * side, dy) for dy in far],
            )
        )
    pick_start = [sum(len(p[1]) for p in plan[:k]) * SLOT for k in range(len(plan))]
    stage_start = [sum(len(p[1]) - 1 for p in plan[:k]) * SLOT for k in range(len(plan))]

    lane = lax.broadcasted_iota(jnp.int32, (SLOT, 128), 1)
    row_number = lax.broadcasted_iota(jnp.int32, (SLOT, rows), 1).astype(f32)

    def build(k, ref):
        known = ref[...]
        for n, (dz, dy) in enumerate(plan[k][1]):
            wanted = jnp.sum(
                jnp.where(lane == part(dz, dy), known, 0.0), axis=1, keepdims=True
            )
            picks[pick_start[k] + n * SLOT : pick_start[k] + (n + 1) * SLOT, :] = jnp.where(
                row_number == wanted, 1.0, 0.0
            ).astype(bf16)

    def halo_rows(sender):
        low = pl.multiple_of(sender % 2 * SLOT, SLOT)
        return own + sender // 2, pl.ds(low, SLOT)

    def extract(c, k, table):
        sender_dz, dests = plan[k]
        sender = part(sender_dz)
        size = len(dests) * SLOT
        found = jnp.dot(
            picks[pick_start[k] : pick_start[k] + size, :], table, preferred_element_type=f32
        ).astype(bf16)
        source[c][(*halo_rows(sender), slice(None))] = found[0:SLOT]
        at = stage_start[k]
        staged[c][at : at + size - SLOT, :] = found[SLOT:]
        for n, (dz, dy) in enumerate(dests[1:]):
            go(
                remote(
                    staged[c].at[at + n * SLOT : at + (n + 1) * SLOT],
                    source[c].at[halo_rows(sender)],
                    halo_send.at[c], halo_recv.at[c], (part(dz, dy), attn),
                )
            )

    def first_hop(c):
        extract(c, 0, source[c][0:own].reshape(rows, CHUNKS[c]))
        for k in range(2):
            if c == 0:
                slot_copy(k, slots).wait_recv()
                go(slot_copy(k + 2, slots_in.at[k]))
            table_copy(c, k, source[c].at[0:own]).wait_recv()
            go(table_copy(c, k + 2, tables[c].at[k]))
        if c + AHEAD < count:
            send_own(c + AHEAD)
        for k in range(2):
            if c == 0:
                build(k + 1, slots_in.at[k])
            extract(c, k + 1, tables[c][k].reshape(rows, CHUNKS[c]))

    def second_hop(c):
        for k in range(2, 4):
            if c == 0:
                slot_copy(k, slots).wait_recv()
                build(k + 1, slots_in.at[k])
            table_copy(c, k, source[c].at[0:own]).wait_recv()
            extract(c, k + 1, tables[c][k].reshape(rows, CHUNKS[c]))

    def slot_rows(owner, low=0, high=None):
        high = rows if high is None else high
        return pl.ds(pl.multiple_of(owner * rows + low, BLOCK), high - low)

    half = rows // 2
    pieces = [(0, 0, rows), (0, 0, rows), (-1, 0, half), (1, half, rows)]

    def ring_copy(c, k):
        dx, low, high = pieces[k]
        at = gathered[c].at[slot_rows(peer(dx), low, high)]
        return remote(at, at, ring_send.at[c, k], ring_recv.at[c, k], (graph, peer(ring[k % 2])))

    def pair_copy(c, k):
        at = gathered[c].at[slot_rows(peer((0, -1, 1, 2)[k]))]
        return remote(at, at, pair_send.at[c, k], pair_recv.at[c, k], (graph, peer(0, 1)))

    def blend(c):
        remote(
            staged[c], staged[c],
            halo_send.at[c], halo_recv.at[c], (graph, peer(0, 1)),
        ).wait_recv()
        for b in range(rows // BLOCK):
            chosen = [source[c][blocks_ref[b, n]] for n in range(blocks_ref.shape[1])]
            here = slice(b * BLOCK, (b + 1) * BLOCK)
            mixed = jnp.dot(
                weights[here, :], jnp.concatenate(chosen, axis=0), preferred_element_type=f32
            )
            mixed = mixed + source[c][b].astype(f32)
            mixed = (mixed * scale[here, 0:1]).astype(bf16)
            own_out[here, starts[c] : starts[c] + CHUNKS[c]] = mixed
            gathered[c][
                pl.ds(pl.multiple_of(attn * rows + b * BLOCK, BLOCK), BLOCK), :
            ] = mixed
        go(ring_copy(c, 0))
        go(ring_copy(c, 1))
        go(pair_copy(c, 0))

    def pass_on(c):
        for k in range(2):
            ring_copy(c, k).wait_recv()
            go(ring_copy(c, k + 2))
            go(pair_copy(c, k + 1))

    def pass_last(c):
        for k in range(2, 4):
            ring_copy(c, k).wait_recv()
        go(pair_copy(c, 3))

    def project(c):
        for k in range(4):
            pair_copy(c, k).wait_recv()

        def one(owner, carry):
            at = slot_rows(owner)
            values = gathered[c][at, :]
            made = jnp.dot(
                values, folded[starts[c] : starts[c] + CHUNKS[c], :], preferred_element_type=f32
            )
            wide = values.astype(f32)
            wide = wide * wide
            squared = sum(wide[:, i : i + 128] for i in range(0, CHUNKS[c], 128))
            if c > 0:
                made = made + total[at, :]
                squared = squared + squares[at, :]
            if c + 1 < count:
                total[at, :] = made
                squares[at, :] = squared
            else:
                mean = jnp.sum(squared, axis=1, keepdims=True) * (1.0 / sum(CHUNKS))
                joined[at, :] = (made * lax.rsqrt(mean + EPSILON)).astype(bf16)
            return carry

        lax.fori_loop(0, 2 * NX, one, 0)

    build(0, slots)
    for c in range(count):
        first_hop(c)
        if c == 0:
            for b in range(edges.shape[0]):
                here = slice(b * BLOCK, (b + 1) * BLOCK)
                degree = jnp.zeros((BLOCK, BLOCK), f32)
                for n in range(edges.shape[1]):
                    value = edges[b, n].astype(f32)
                    degree = degree + value
                    weights[here, n * BLOCK : (n + 1) * BLOCK] = value.astype(bf16)
                degree = jnp.sum(degree, axis=1, keepdims=True)
                scale[here, :] = jnp.broadcast_to(lax.rsqrt(1.0 + degree), (BLOCK, BLOCK))
            for k, load in enumerate(loads):
                load.wait()
                folded[:, k * width : (k + 1) * width] = (
                    columns[k].astype(f32) * gain[...]
                ).astype(bf16)
        if c >= 2:
            pass_last(c - 2)
        if c >= 1:
            blend(c - 1)
        if c >= 2:
            project(c - 2)
        second_hop(c)
        if c >= 1:
            pass_on(c - 1)
    if count >= 2:
        pass_last(count - 2)
    blend(count - 1)
    if count >= 2:
        project(count - 2)
    pass_on(count - 1)
    pass_last(count - 1)
    project(count - 1)

    for k in range(4):
        slot_copy(k, slots).wait_send()
    for c in range(count):
        for k in range(4):
            table_copy(c, k, source[c].at[0:own]).wait_send()
            ring_copy(c, k).wait_send()
            pair_copy(c, k).wait_send()
        remote(
            staged[c], staged[c],
            halo_send.at[c], halo_recv.at[c], (graph, peer(0, 1)),
        ).wait_send()


def spread(features, slots, edge_blocks, edge_weight, gain, query_weight, key_weight, value_weight):
    rows, model = features.shape
    members = 2 * NX
    width = 2 * HEAD_DIM
    nb = edge_blocks.shape[1]
    count = len(CHUNKS)
    vmem = pl.BlockSpec(memory_space=pltpu.VMEM)
    smem = pl.BlockSpec(memory_space=pltpu.SMEM)
    hbm = pl.BlockSpec(memory_space=pl.ANY)
    arriving = (NZ * NY - 5) * SLOT
    own = rows // BLOCK
    sources = own + NZ * NY * SLOT // BLOCK
    scratch = [pltpu.VMEM((sources, BLOCK, w), bf16) for w in CHUNKS]
    scratch += [pltpu.VMEM((4, own, BLOCK, w), bf16) for w in CHUNKS]
    scratch += [pltpu.VMEM((arriving, w), bf16) for w in CHUNKS]
    scratch += [pltpu.VMEM((members * rows, w), bf16) for w in CHUNKS]
    scratch += [
        pltpu.VMEM((4, SLOT, 128), f32),
        pltpu.VMEM((NZ * NY * SLOT, rows), bf16),
        pltpu.VMEM((rows, nb * BLOCK), bf16),
        pltpu.VMEM((rows, BLOCK), f32),
        pltpu.VMEM((3, model, width), bf16),
        pltpu.VMEM((model, 3 * width), bf16),
        pltpu.VMEM((members * rows, 3 * width), f32),
        pltpu.VMEM((members * rows, 128), f32),
        pltpu.SemaphoreType.DMA((3,)),
        pltpu.SemaphoreType.DMA((4,)),
        pltpu.SemaphoreType.DMA((4,)),
        pltpu.SemaphoreType.DMA((count, 4)),
        pltpu.SemaphoreType.DMA((count, 4)),
        pltpu.SemaphoreType.DMA((count,)),
        pltpu.SemaphoreType.DMA((count,)),
        pltpu.SemaphoreType.DMA((count, 4)),
        pltpu.SemaphoreType.DMA((count, 4)),
        pltpu.SemaphoreType.DMA((count, 4)),
        pltpu.SemaphoreType.DMA((count, 4)),
    ]
    return pl.pallas_call(
        spread_kernel,
        out_shape=(
            jax.ShapeDtypeStruct((members * rows, 3 * width), bf16),
            jax.ShapeDtypeStruct((rows, model), bf16),
        ),
        in_specs=[vmem, vmem, smem, vmem, vmem, hbm, hbm, hbm],
        out_specs=(vmem, vmem),
        scratch_shapes=scratch,
        compiler_params=pltpu.CompilerParams(
            collective_id=1, has_side_effects=True, vmem_limit_bytes=58 * 2**20
        ),
        name="spread",
    )(
        features, slots, edge_blocks, edge_weight, gain.reshape(model, 1),
        query_weight, key_weight, value_weight,
    )


def attend_kernel(mask_ref, joined_ref, out_ref, scores_a, scores_b):
    width = 2 * HEAD_DIM
    blocks, keys = mask_ref.shape
    first = lax.broadcasted_iota(jnp.int32, (BLOCK, width), 1) < HEAD_DIM
    ones = jnp.ones((2 * BLOCK, width), jnp.bfloat16)

    def rows_of(block):
        return pl.ds(pl.multiple_of(block * BLOCK, BLOCK), BLOCK)

    def pair(block, step, column):
        cols = slice(column * width, (column + 1) * width)
        low = joined_ref[rows_of(mask_ref[block, 2 * step]), cols]
        high = joined_ref[rows_of(mask_ref[block, 2 * step + 1]), cols]
        return jnp.concatenate([low, high], axis=0)

    def score(block, scores):
        query = joined_ref[rows_of(block), 0:width] * jnp.bfloat16(HEAD_DIM ** (-0.5))
        zero = jnp.zeros_like(query)
        query = jnp.concatenate(
            [jnp.where(first, query, zero), jnp.where(first, zero, query)], axis=0
        )
        top = None
        for step in range(keys // 2):
            part = lax.dot_general(
                query, pair(block, step, 1), (((1,), (1,)), ((), ())),
                preferred_element_type=jnp.float32,
            )
            scores[:, 2 * step * BLOCK : (2 * step + 2) * BLOCK] = part
            part = jnp.maximum(part[:, :BLOCK], part[:, BLOCK:])
            top = part if top is None else jnp.maximum(top, part)
        return jnp.max(top, axis=1, keepdims=True)

    def mix(block, scores, top):
        total = jnp.zeros((2 * BLOCK, 2 * width), jnp.float32)
        for step in range(keys // 2):
            values = jnp.concatenate([pair(block, step, 2), ones], axis=1)
            part = scores[:, 2 * step * BLOCK : (2 * step + 2) * BLOCK]
            raised = jnp.exp(part - top).astype(jnp.bfloat16)
            total = total + jnp.dot(raised, values, preferred_element_type=jnp.float32)
        result = total[:, :width] / total[:, width:]
        out_ref[rows_of(block), :] = jnp.where(first, result[:BLOCK], result[BLOCK:]).astype(
            jnp.bfloat16
        )

    def two(index, carry):
        top_a = score(2 * index, scores_a)
        top_b = score(2 * index + 1, scores_b)
        mix(2 * index, scores_a, top_a)
        mix(2 * index + 1, scores_b, top_b)
        return carry

    lax.fori_loop(0, blocks // 2, two, 0)


def attend_blocks(joined, mask):
    keys = mask.shape[1] * BLOCK
    return pl.pallas_call(
        attend_kernel,
        out_shape=jax.ShapeDtypeStruct((joined.shape[0], 2 * HEAD_DIM), jnp.bfloat16),
        in_specs=[
            pl.BlockSpec(memory_space=pltpu.SMEM),
            pl.BlockSpec(memory_space=pltpu.VMEM),
        ],
        out_specs=pl.BlockSpec(memory_space=pltpu.VMEM),
        scratch_shapes=[pltpu.VMEM((2 * BLOCK, keys), jnp.float32)] * 2,
        compiler_params=pltpu.CompilerParams(vmem_limit_bytes=40 * 2**20),
    )(mask, joined)


def on_device(
    features,
    send_rows,
    send_count,
    edge_blocks,
    edge_weight,
    mask_blocks,
    norm_gain,
    query_weight,
    key_weight,
    value_weight,
    out_weight,
):
    slot = jnp.arange(SLOT, dtype=jnp.int32)[:, None]
    slots = jnp.where(slot < send_count, send_rows[0].T, -1).astype(f32)
    slots = jnp.pad(slots, ((0, 0), (0, 128 - slots.shape[1])))
    joined, aggregated = spread(
        features, slots, edge_blocks, edge_weight, norm_gain, query_weight, key_weight, value_weight
    )
    attended = attend_blocks(joined, mask_blocks[0])
    returned = lax.all_to_all(attended, "attn", split_axis=0, concat_axis=1, tiled=True)
    updated = jnp.dot(returned, out_weight, preferred_element_type=f32) + aggregated.astype(f32)
    return updated.astype(bf16)


def solution(mesh):
    placed = (
        P(("graph", "attn"), None),
        P(("graph", "attn"), None, None),
        P(("graph", "attn"), None),
        P(("graph", "attn"), None),
        P(("graph", "attn"), None, None, None),
        P("graph", None, None),
        P(),
        P(),
        P(),
        P(),
        P(),
    )
    return jax.shard_map(
        on_device, mesh=mesh, in_specs=placed, out_specs=P(("graph", "attn"), None), check_vma=False
    )
```

```python
import jax
import jax.numpy as jnp
from jax import lax
from jax.experimental import pallas as pl
from jax.experimental.pallas import tpu as pltpu
from jax.sharding import PartitionSpec as P

HEAD_DIM = 64
BLOCK = 128
EPSILON = 1e-06
SCORE_SCALE = HEAD_DIM ** (-0.5) * 1.4426950408889634
NZ = 8
NY = 4
NX = 4
SLOT = 64
CHUNKS = (256, 256, 256, 256)
AHEAD = 1
PLUS = (0, 1)
MINUS = (2, 3)
f32 = jnp.float32
bf16 = jnp.bfloat16


def layer_kernel(
    features, send_rows, send_count, blocks_ref, mask_ref, gain, edges_hbm,
    query_hbm, key_hbm, value_hbm, out_hbm, result, *scratch,
):
    count = len(CHUNKS)
    starts = [sum(CHUNKS[:c]) for c in range(count)]
    scratch = list(scratch)
    source = [scratch.pop(0) for _ in range(count)]
    tables = [scratch.pop(0) for _ in range(count)]
    staged = [scratch.pop(0) for _ in range(count)]
    gathered = [scratch.pop(0) for _ in range(count)]
    (
        feature_sem, slots, slots_in, edges, picks, weights, scale, columns, folded, out_weight, total, squares,
        own_out, joined, scores_a, scores_b, mixed_out, mixed_in,
        column_sem, mixed_send, mixed_recv, slot_send, slot_recv, table_send, table_recv, halo_send, halo_recv,
        ring_send, ring_recv, pair_send, pair_recv,
    ) = scratch
    own = features.shape[0]
    rows = own * BLOCK
    graph = lax.axis_index("graph")
    attn = lax.axis_index("attn")
    z, y = graph // NY, graph % NY
    x, core = attn // 2, attn % 2

    def part(dz, dy=0):
        return lax.rem(z + dz + NZ, NZ) * NY + lax.rem(y + dy, NY)

    def peer(dx, flip=0):
        return lax.rem(x + dx + NX, NX) * 2 + (core if flip == 0 else 1 - core)

    def remote(src, dst, send, recv, to):
        return pltpu.make_async_remote_copy(
            src_ref=src, dst_ref=dst, send_sem=send, recv_sem=recv,
            device_id=to, device_id_type=pl.DeviceIdType.MESH,
        )

    width = 2 * HEAD_DIM
    first_col = pl.multiple_of(attn * width, width)
    loads = [
        pltpu.make_async_copy(
            ref.at[:, pl.ds(first_col, width)], columns.at[k], column_sem.at[k]
        )
        for k, ref in enumerate((query_hbm, key_hbm, value_hbm))
    ]
    loads.append(pltpu.make_async_copy(edges_hbm, edges, column_sem.at[3]))
    loads.append(pltpu.make_async_copy(out_hbm, out_weight, column_sem.at[4]))
    feature_loads = [
        pltpu.make_async_copy(
            features.at[:, :, pl.ds(starts[c], CHUNKS[c])], source[c].at[0:own], feature_sem.at[c]
        )
        for c in range(count)
    ]
    for load in feature_loads + loads:
        load.start()
    barrier = pltpu.get_barrier_semaphore()
    near = {(0, dy) for dy in range(1, NY)}
    near |= {(dz, dy) for dz in (1, -1) for dy in range(NY)}
    for dy in PLUS:
        near |= {(2, dy), (-2, -dy % NY)}
    for dy in MINUS:
        near |= {(-2, dy), (2, -dy % NY)}
    near = sorted(near)
    greeted = [(part(dz, dy), attn) for dz, dy in near]
    greeted += [(graph, peer(1)), (graph, peer(-1)), (graph, peer(0, 1))]
    greeted += [(graph, peer(2)), (graph, peer(1, 1)), (graph, peer(-1, 1)), (graph, peer(2, 1))]
    for device in greeted:
        pl.semaphore_signal(barrier, inc=1, device_id=device, device_id_type=pl.DeviceIdType.MESH)
    slots[...] = jnp.full((BLOCK, BLOCK), -1.0, f32)
    slots[0 : NZ * NY, 0:SLOT] = send_rows[...].astype(f32)
    turned = slots[...].T
    slots[...] = jnp.zeros((BLOCK, BLOCK), f32)
    slots[0:1, 0 : NZ * NY] = send_count[...].astype(f32)
    place = lax.broadcasted_iota(jnp.int32, (BLOCK, BLOCK), 0).astype(f32)
    slots[...] = jnp.where(place < slots[0:1, :], turned, -1.0)
    pl.semaphore_wait(barrier, len(greeted))

    def go(copy):
        copy.start()

    ring = [1, -1]

    def slot_copy(k, src):
        return remote(
            src, slots_in.at[k], slot_send.at[k], slot_recv.at[k], (part(ring[k % 2]), attn)
        )

    def table_copy(c, k, src):
        return remote(
            src, tables[c].at[k], table_send.at[c, k], table_recv.at[c, k],
            (part(ring[k % 2]), attn),
        )

    def send_own(c):
        feature_loads[c].wait()
        for k in range(2):
            go(table_copy(c, k, source[c].at[0:own]))

    for k in range(2):
        go(slot_copy(k, slots.at[0:SLOT]))
    for c in range(AHEAD):
        send_own(c)

    plan = [(0, [(0, dy) for dy in range(NY)])]
    for side in (1, -1):
        plan.append((-side, [(0, dy) for dy in range(NY)]))
    for side, far in ((1, PLUS), (-1, MINUS)):
        plan.append(
            (
                -2 * side,
                [(0, dy) for dy in range(NY)]
                + [(side, dy) for dy in range(NY)]
                + [(2 * side, dy) for dy in far],
            )
        )
    pick_start = [sum(len(p[1]) for p in plan[:k]) * SLOT for k in range(len(plan))]
    stage_start = [sum(len(p[1]) - 1 for p in plan[:k]) * SLOT for k in range(len(plan))]

    lane = lax.broadcasted_iota(jnp.int32, (SLOT, 128), 1)
    row_number = lax.broadcasted_iota(jnp.int32, (SLOT, rows), 1).astype(f32)

    def build(k, ref):
        known = ref[...]
        for n, (dz, dy) in enumerate(plan[k][1]):
            wanted = jnp.sum(
                jnp.where(lane == part(dz, dy), known, 0.0), axis=1, keepdims=True
            )
            picks[pick_start[k] + n * SLOT : pick_start[k] + (n + 1) * SLOT, :] = jnp.where(
                row_number == wanted, 1.0, 0.0
            ).astype(bf16)

    def halo_rows(sender):
        low = pl.multiple_of(sender % 2 * SLOT, SLOT)
        return own + sender // 2, pl.ds(low, SLOT)

    def extract(c, k, table):
        sender_dz, dests = plan[k]
        sender = part(sender_dz)
        size = len(dests) * SLOT
        found = jnp.dot(
            picks[pick_start[k] : pick_start[k] + size, :], table, preferred_element_type=f32
        ).astype(bf16)
        source[c][(*halo_rows(sender), slice(None))] = found[0:SLOT]
        at = stage_start[k]
        staged[c][at : at + size - SLOT, :] = found[SLOT:]
        for n, (dz, dy) in enumerate(dests[1:]):
            go(
                remote(
                    staged[c].at[at + n * SLOT : at + (n + 1) * SLOT],
                    source[c].at[halo_rows(sender)],
                    halo_send.at[c], halo_recv.at[c], (part(dz, dy), attn),
                )
            )

    def first_hop(c):
        extract(c, 0, source[c][0:own].reshape(rows, CHUNKS[c]))
        for k in range(2):
            if c == 0:
                slot_copy(k, slots.at[0:SLOT]).wait_recv()
                go(slot_copy(k + 2, slots_in.at[k]))
            table_copy(c, k, source[c].at[0:own]).wait_recv()
            go(table_copy(c, k + 2, tables[c].at[k]))
        if c + AHEAD < count:
            send_own(c + AHEAD)
        for k in range(2):
            if c == 0:
                build(k + 1, slots_in.at[k])
            extract(c, k + 1, tables[c][k].reshape(rows, CHUNKS[c]))

    def second_hop(c):
        for k in range(2, 4):
            if c == 0:
                slot_copy(k, slots.at[0:SLOT]).wait_recv()
                build(k + 1, slots_in.at[k])
            table_copy(c, k, source[c].at[0:own]).wait_recv()
            extract(c, k + 1, tables[c][k].reshape(rows, CHUNKS[c]))

    def slot_rows(owner, low=0, high=None):
        high = rows if high is None else high
        return pl.ds(pl.multiple_of(owner * rows + low, BLOCK), high - low)

    half = rows // 2
    pieces = [(0, 0, rows), (0, 0, rows), (-1, 0, half), (1, half, rows)]

    def ring_copy(c, k):
        dx, low, high = pieces[k]
        at = gathered[c].at[slot_rows(peer(dx), low, high)]
        return remote(at, at, ring_send.at[c, k], ring_recv.at[c, k], (graph, peer(ring[k % 2])))

    def pair_copy(c, k):
        at = gathered[c].at[slot_rows(peer((0, -1, 1, 2)[k]))]
        return remote(at, at, pair_send.at[c, k], pair_recv.at[c, k], (graph, peer(0, 1)))

    def blend(c):
        remote(
            staged[c], staged[c],
            halo_send.at[c], halo_recv.at[c], (graph, peer(0, 1)),
        ).wait_recv()
        for b in range(rows // BLOCK):
            chosen = [source[c][blocks_ref[b, n]] for n in range(blocks_ref.shape[1])]
            here = slice(b * BLOCK, (b + 1) * BLOCK)
            mixed = jnp.dot(
                weights[here, :], jnp.concatenate(chosen, axis=0), preferred_element_type=f32
            )
            mixed = mixed + source[c][b].astype(f32)
            mixed = (mixed * scale[here, 0:1]).astype(bf16)
            own_out[here, starts[c] : starts[c] + CHUNKS[c]] = mixed
            gathered[c][
                pl.ds(pl.multiple_of(attn * rows + b * BLOCK, BLOCK), BLOCK), :
            ] = mixed
        go(ring_copy(c, 0))
        go(ring_copy(c, 1))
        go(pair_copy(c, 0))

    def pass_on(c):
        for k in range(2):
            ring_copy(c, k).wait_recv()
            go(ring_copy(c, k + 2))
            go(pair_copy(c, k + 1))

    def pass_last(c):
        for k in range(2, 4):
            ring_copy(c, k).wait_recv()
        go(pair_copy(c, 3))

    def project(c):
        for k in range(4):
            pair_copy(c, k).wait_recv()

        def one(owner, carry):
            at = slot_rows(owner)
            values = gathered[c][at, :]
            made = jnp.dot(
                values, folded[starts[c] : starts[c] + CHUNKS[c], :], preferred_element_type=f32
            )
            wide = values.astype(f32)
            wide = wide * wide
            squared = sum(wide[:, i : i + 128] for i in range(0, CHUNKS[c], 128))
            if c > 0:
                made = made + total[at, :]
                squared = squared + squares[at, :]
            if c + 1 < count:
                total[at, :] = made
                squares[at, :] = squared
            else:
                mean = jnp.sum(squared, axis=1, keepdims=True) * (1.0 / sum(CHUNKS))
                made = (made * lax.rsqrt(mean + EPSILON)).astype(bf16)
                for k in range(3):
                    joined[k, pl.ds(owner * own, own)] = made[
                        :, k * width : (k + 1) * width
                    ].reshape(own, BLOCK, width)
            return carry

        lax.fori_loop(0, 2 * NX, one, 0)

    build(0, slots.at[0:SLOT])
    for c in range(count):
        first_hop(c)
        if c == 0:
            loads[3].wait()
            for b in range(edges.shape[0]):
                here = slice(b * BLOCK, (b + 1) * BLOCK)
                degree = jnp.zeros((BLOCK, BLOCK), f32)
                for n in range(edges.shape[1]):
                    value = edges[b, n].astype(f32)
                    degree = degree + value
                    weights[here, n * BLOCK : (n + 1) * BLOCK] = value.astype(bf16)
                degree = jnp.sum(degree, axis=1, keepdims=True)
                scale[here, :] = jnp.broadcast_to(lax.rsqrt(1.0 + degree), (BLOCK, BLOCK))
            for load in loads[:3]:
                load.wait()
            for i in range(gain.shape[0]):
                here = slice(i * 128, (i + 1) * 128)
                factor = jnp.broadcast_to(gain[i : i + 1, :], (128, 128)).T
                for k in range(3):
                    raised = factor * SCORE_SCALE if k == 0 else factor
                    folded[here, k * width : (k + 1) * width] = (
                        columns[k, here, :].astype(f32) * raised
                    ).astype(bf16)
        if c >= 2:
            pass_last(c - 2)
        if c >= 1:
            blend(c - 1)
        if c >= 2:
            project(c - 2)
        second_hop(c)
        if c >= 1:
            pass_on(c - 1)
    if count >= 2:
        pass_last(count - 2)
    blend(count - 1)
    if count >= 2:
        project(count - 2)
    pass_on(count - 1)
    pass_last(count - 1)
    project(count - 1)

    first = lax.broadcasted_iota(jnp.int32, (BLOCK, width), 1) < HEAD_DIM
    ones = jnp.ones((2 * BLOCK, width), bf16)
    keys = mask_ref.shape[0]

    def pair(block, step, kind):
        low = joined[kind, mask_ref[2 * step, block]]
        high = joined[kind, mask_ref[2 * step + 1, block]]
        return jnp.concatenate([low, high], axis=0)

    def score(block, scores):
        query = joined[0, block]
        zero = jnp.zeros_like(query)
        query = jnp.concatenate(
            [jnp.where(first, query, zero), jnp.where(first, zero, query)], axis=0
        )
        top = None
        for step in range(keys // 2):
            piece = lax.dot_general(
                query, pair(block, step, 1), (((1,), (1,)), ((), ())), preferred_element_type=f32
            )
            scores[:, 2 * step * BLOCK : (2 * step + 2) * BLOCK] = piece
            piece = jnp.maximum(piece[:, :BLOCK], piece[:, BLOCK:])
            top = piece if top is None else jnp.maximum(top, piece)
        return jnp.max(top, axis=1, keepdims=True)

    def mix(block, scores, top):
        sums = jnp.zeros((2 * BLOCK, 2 * width), f32)
        for step in range(keys // 2):
            values = jnp.concatenate([pair(block, step, 2), ones], axis=1)
            piece = scores[:, 2 * step * BLOCK : (2 * step + 2) * BLOCK]
            raised = jnp.exp2(piece - top).astype(bf16)
            sums = sums + jnp.dot(raised, values, preferred_element_type=f32)
        sums = sums[:, :width] / sums[:, width:]
        return jnp.where(first, sums[:BLOCK], sums[BLOCK:]).astype(bf16)

    def mixed_copy(owner, low):
        return remote(
            mixed_out.at[pl.ds(pl.multiple_of(owner * rows + low, BLOCK), 2 * BLOCK)],
            mixed_in.at[attn, pl.ds(pl.multiple_of(low, BLOCK), 2 * BLOCK)],
            mixed_send, mixed_recv, (graph, owner),
        )

    def attend(index):
        owner = lax.rem(attn + 1 + index // 2, 2 * NX)
        low = lax.rem(index, 2) * (2 * BLOCK)
        block = owner * own + lax.rem(index, 2) * 2
        top_a = score(block, scores_a)
        top_b = score(block + 1, scores_b)
        low_rows = mix(block, scores_a, top_a)
        high_rows = mix(block + 1, scores_b, top_b)
        return owner, low, low_rows, high_rows

    def away(index, carry):
        owner, low, low_rows, high_rows = attend(index)
        at = pl.multiple_of(owner * rows + low, BLOCK)
        mixed_out[pl.ds(at, BLOCK), :] = low_rows
        mixed_out[pl.ds(pl.multiple_of(at + BLOCK, BLOCK), BLOCK), :] = high_rows
        mixed_copy(owner, low).start()
        return carry

    def home(index, carry):
        owner, low, low_rows, high_rows = attend(index)
        at = pl.multiple_of(low, BLOCK)
        mixed_in[attn, pl.ds(at, BLOCK), :] = low_rows
        mixed_in[attn, pl.ds(pl.multiple_of(at + BLOCK, BLOCK), BLOCK), :] = high_rows
        return carry

    lax.fori_loop(0, 4 * NX - 2, away, 0)
    lax.fori_loop(4 * NX - 2, 4 * NX, home, 0)
    returned = remote(
        mixed_out.at[0 : (2 * NX - 1) * rows], mixed_out.at[0 : (2 * NX - 1) * rows],
        mixed_send, mixed_recv, (graph, peer(0, 1)),
    )
    loads[4].wait()
    returned.wait_recv()
    for b in range(own):
        here = slice(b * BLOCK, (b + 1) * BLOCK)
        attended = jnp.concatenate([mixed_in[k, here, :] for k in range(2 * NX)], axis=1)
        made = jnp.dot(attended, out_weight[...], preferred_element_type=f32)
        result[here, :] = (made + own_out[here, :].astype(f32)).astype(bf16)

    returned.wait_send()
    for k in range(4):
        slot_copy(k, slots.at[0:SLOT]).wait_send()
    for c in range(count):
        for k in range(4):
            table_copy(c, k, source[c].at[0:own]).wait_send()
            ring_copy(c, k).wait_send()
            pair_copy(c, k).wait_send()
        remote(
            staged[c], staged[c],
            halo_send.at[c], halo_recv.at[c], (graph, peer(0, 1)),
        ).wait_send()


def on_device(
    features,
    send_rows,
    send_count,
    edge_blocks,
    edge_weight,
    mask_blocks,
    norm_gain,
    query_weight,
    key_weight,
    value_weight,
    out_weight,
):
    rows, model = features.shape
    members = 2 * NX
    width = 2 * HEAD_DIM
    keys = mask_blocks.shape[2] * BLOCK
    nb = edge_blocks.shape[1]
    count = len(CHUNKS)
    own = rows // BLOCK
    sources = own + NZ * NY * SLOT // BLOCK
    arriving = (NZ * NY - 5) * SLOT
    vmem = pl.BlockSpec(memory_space=pltpu.VMEM)
    smem = pl.BlockSpec(memory_space=pltpu.SMEM)
    hbm = pl.BlockSpec(memory_space=pl.ANY)
    scratch = [pltpu.VMEM((sources, BLOCK, w), bf16) for w in CHUNKS]
    scratch += [pltpu.VMEM((4, own, BLOCK, w), bf16) for w in CHUNKS]
    scratch += [pltpu.VMEM((arriving, w), bf16) for w in CHUNKS]
    scratch += [pltpu.VMEM((members * rows, w), bf16) for w in CHUNKS]
    scratch += [
        pltpu.SemaphoreType.DMA((count,)),
        pltpu.VMEM((BLOCK, BLOCK), f32),
        pltpu.VMEM((4, SLOT, 128), f32),
        pltpu.VMEM(edge_weight.shape, jnp.int32),
        pltpu.VMEM((NZ * NY * SLOT, rows), bf16),
        pltpu.VMEM((rows, nb * BLOCK), bf16),
        pltpu.VMEM((rows, BLOCK), f32),
        pltpu.VMEM((3, model, width), bf16),
        pltpu.VMEM((model, 3 * width), bf16),
        pltpu.VMEM((model, model), bf16),
        pltpu.VMEM((members * rows, 3 * width), f32),
        pltpu.VMEM((members * rows, 128), f32),
        pltpu.VMEM((rows, model), bf16),
        pltpu.VMEM((3, members * own, BLOCK, width), bf16),
        pltpu.VMEM((2 * BLOCK, keys), f32),
        pltpu.VMEM((2 * BLOCK, keys), f32),
        pltpu.VMEM((members * rows, width), bf16),
        pltpu.VMEM((members, rows, width), bf16),
        pltpu.SemaphoreType.DMA((5,)),
        pltpu.SemaphoreType.DMA,
        pltpu.SemaphoreType.DMA,
        pltpu.SemaphoreType.DMA((4,)),
        pltpu.SemaphoreType.DMA((4,)),
        pltpu.SemaphoreType.DMA((count, 4)),
        pltpu.SemaphoreType.DMA((count, 4)),
        pltpu.SemaphoreType.DMA((count,)),
        pltpu.SemaphoreType.DMA((count,)),
        pltpu.SemaphoreType.DMA((count, 4)),
        pltpu.SemaphoreType.DMA((count, 4)),
        pltpu.SemaphoreType.DMA((count, 4)),
        pltpu.SemaphoreType.DMA((count, 4)),
    ]
    return pl.pallas_call(
        layer_kernel,
        out_shape=jax.ShapeDtypeStruct((rows, model), bf16),
        in_specs=[hbm, vmem, vmem, smem, smem, vmem, hbm, hbm, hbm, hbm, hbm],
        out_specs=vmem,
        scratch_shapes=scratch,
        compiler_params=pltpu.CompilerParams(
            collective_id=1, has_side_effects=True, vmem_limit_bytes=60 * 2**20
        ),
        name="layer",
    )(
        features.reshape(own, BLOCK, model), send_rows[0], send_count, edge_blocks,
        mask_blocks[0].T, norm_gain.reshape(-1, 128), edge_weight,
        query_weight, key_weight, value_weight, out_weight,
    )


def solution(mesh):
    placed = (
        P(("graph", "attn"), None),
        P(("graph", "attn"), None, None),
        P(("graph", "attn"), None),
        P(("graph", "attn"), None),
        P(("graph", "attn"), None, None, None),
        P("graph", None, None),
        P(),
        P(),
        P(),
        P(),
        P(),
    )
    return jax.shard_map(
        on_device, mesh=mesh, in_specs=placed, out_specs=P(("graph", "attn"), None), check_vma=False
    )
```

```python
import jax
import jax.numpy as jnp
from jax import lax
from jax.experimental import pallas as pl
from jax.experimental.pallas import tpu as pltpu
from jax.sharding import PartitionSpec as P

HEAD_DIM = 64
BLOCK = 128
EPSILON = 1e-06
SCORE_SCALE = HEAD_DIM ** (-0.5) * 1.4426950408889634
NZ = 8
NY = 4
NX = 4
SLOT = 64
CHUNKS = (512, 256, 256)
AHEAD = 1
PLUS = (0, 1)
MINUS = (2, 3)
f32 = jnp.float32
bf16 = jnp.bfloat16


def layer_kernel(
    features, send_rows, send_count, blocks_ref, mask_ref, gain, edges_hbm,
    query_hbm, key_hbm, value_hbm, mixed_hbm, own_hbm, *scratch,
):
    count = len(CHUNKS)
    starts = [sum(CHUNKS[:c]) for c in range(count)]
    scratch = list(scratch)
    source = [scratch.pop(0) for _ in range(count)]
    tables = [scratch.pop(0) for _ in range(count)]
    staged = [scratch.pop(0) for _ in range(count)]
    gathered = [scratch.pop(0) for _ in range(count)]
    (
        feature_sem, slots, slots_in, edges, picks, weights, scale, columns, folded, total, squares,
        own_out, joined, scores_a, scores_b, mixed_out, mixed_in,
        column_sem, mixed_send, mixed_recv, slot_send, slot_recv, table_send, table_recv, halo_send, halo_recv,
        ring_send, ring_recv, pair_send, pair_recv,
    ) = scratch
    own = features.shape[0]
    rows = own * BLOCK
    graph = lax.axis_index("graph")
    attn = lax.axis_index("attn")
    z, y = graph // NY, graph % NY
    x, core = attn // 2, attn % 2

    def part(dz, dy=0):
        return lax.rem(z + dz + NZ, NZ) * NY + lax.rem(y + dy, NY)

    def peer(dx, flip=0):
        return lax.rem(x + dx + NX, NX) * 2 + (core if flip == 0 else 1 - core)

    def remote(src, dst, send, recv, to):
        return pltpu.make_async_remote_copy(
            src_ref=src, dst_ref=dst, send_sem=send, recv_sem=recv,
            device_id=to, device_id_type=pl.DeviceIdType.MESH,
        )

    width = 2 * HEAD_DIM
    first_col = pl.multiple_of(attn * width, width)
    loads = [
        pltpu.make_async_copy(
            ref.at[:, pl.ds(first_col, width)], columns.at[k], column_sem.at[k]
        )
        for k, ref in enumerate((query_hbm, key_hbm, value_hbm))
    ]
    loads.append(pltpu.make_async_copy(edges_hbm, edges, column_sem.at[3]))
    feature_loads = [
        pltpu.make_async_copy(
            features.at[:, :, pl.ds(starts[c], CHUNKS[c])], source[c].at[0:own], feature_sem.at[c]
        )
        for c in range(count)
    ]
    for load in feature_loads + loads:
        load.start()
    barrier = pltpu.get_barrier_semaphore()
    near = {(0, dy) for dy in range(1, NY)}
    near |= {(dz, dy) for dz in (1, -1) for dy in range(NY)}
    for dy in PLUS:
        near |= {(2, dy), (-2, -dy % NY)}
    for dy in MINUS:
        near |= {(-2, dy), (2, -dy % NY)}
    near = sorted(near)
    greeted = [(part(dz, dy), attn) for dz, dy in near]
    greeted += [(graph, peer(1)), (graph, peer(-1)), (graph, peer(0, 1))]
    greeted += [(graph, peer(2)), (graph, peer(1, 1)), (graph, peer(-1, 1)), (graph, peer(2, 1))]
    for device in greeted:
        pl.semaphore_signal(barrier, inc=1, device_id=device, device_id_type=pl.DeviceIdType.MESH)
    slots[...] = jnp.full((BLOCK, BLOCK), -1.0, f32)
    slots[0 : NZ * NY, 0:SLOT] = send_rows[...].astype(f32)
    turned = slots[...].T
    slots[...] = jnp.zeros((BLOCK, BLOCK), f32)
    slots[0:1, 0 : NZ * NY] = send_count[...].astype(f32)
    place = lax.broadcasted_iota(jnp.int32, (BLOCK, BLOCK), 0).astype(f32)
    slots[...] = jnp.where(place < slots[0:1, :], turned, -1.0)
    pl.semaphore_wait(barrier, len(greeted))

    def go(copy):
        copy.start()

    ring = [1, -1]

    def slot_copy(k, src):
        return remote(
            src, slots_in.at[k], slot_send.at[k], slot_recv.at[k], (part(ring[k % 2]), attn)
        )

    def table_copy(c, k, src):
        return remote(
            src, tables[c].at[k], table_send.at[c, k], table_recv.at[c, k],
            (part(ring[k % 2]), attn),
        )

    def send_own(c):
        feature_loads[c].wait()
        for k in range(2):
            go(table_copy(c, k, source[c].at[0:own]))

    for k in range(2):
        go(slot_copy(k, slots.at[0:SLOT]))
    for c in range(AHEAD):
        send_own(c)

    plan = [(0, [(0, dy) for dy in range(NY)])]
    for side in (1, -1):
        plan.append((-side, [(0, dy) for dy in range(NY)]))
    for side, far in ((1, PLUS), (-1, MINUS)):
        onward = [(side, dy) for dy in range(NY)] + [(2 * side, dy) for dy in far]
        plan.append((-2 * side, onward))
    for side in (1, -1):
        plan.append((-2 * side, [(0, dy) for dy in range(NY)]))
    keeps = [int(p[1][0] == (0, 0)) for p in plan]
    pick_start = [sum(len(p[1]) for p in plan[:k]) * SLOT for k in range(len(plan))]
    stage_start = [pick_start[k] - sum(keeps[:k]) * SLOT for k in range(len(plan))]

    lane = lax.broadcasted_iota(jnp.int32, (SLOT, 128), 1)
    row_number = lax.broadcasted_iota(jnp.int32, (SLOT, rows), 1).astype(f32)

    def build(k, ref):
        known = ref[...]
        for n, (dz, dy) in enumerate(plan[k][1]):
            wanted = jnp.sum(
                jnp.where(lane == part(dz, dy), known, 0.0), axis=1, keepdims=True
            )
            picks[pick_start[k] + n * SLOT : pick_start[k] + (n + 1) * SLOT, :] = jnp.where(
                row_number == wanted, 1.0, 0.0
            ).astype(bf16)

    def halo_rows(sender):
        low = pl.multiple_of(sender % 2 * SLOT, SLOT)
        return own + sender // 2, pl.ds(low, SLOT)

    def extract(c, k, table):
        sender_dz, dests = plan[k]
        sender = part(sender_dz)
        size = len(dests) * SLOT
        found = jnp.dot(
            picks[pick_start[k] : pick_start[k] + size, :], table, preferred_element_type=f32
        ).astype(bf16)
        kept = keeps[k]
        if kept:
            source[c][(*halo_rows(sender), slice(None))] = found[0:SLOT]
        at = stage_start[k]
        staged[c][at : at + size - kept * SLOT, :] = found[kept * SLOT :]
        for n, (dz, dy) in enumerate(dests[kept:]):
            go(
                remote(
                    staged[c].at[at + n * SLOT : at + (n + 1) * SLOT],
                    source[c].at[halo_rows(sender)],
                    halo_send.at[c], halo_recv.at[c], (part(dz, dy), attn),
                )
            )

    def first_hop(c):
        if c == 0:
            extract(c, 0, source[c][0:own].reshape(rows, CHUNKS[c]))
        for k in range(2):
            if c == 0:
                slot_copy(k, slots.at[0:SLOT]).wait_recv()
                go(slot_copy(k + 2, slots_in.at[k]))
            table_copy(c, k, source[c].at[0:own]).wait_recv()
            go(table_copy(c, k + 2, tables[c].at[k]))
        if AHEAD == 1 and c + 1 < count:
            send_own(c + 1)
        if c > 0:
            extract(c, 0, source[c][0:own].reshape(rows, CHUNKS[c]))
        for k in range(2):
            if c == 0:
                build(k + 1, slots_in.at[k])
            extract(c, k + 1, tables[c][k].reshape(rows, CHUNKS[c]))

    def second_hop(c):
        for k in range(2, 4):
            if c == 0:
                slot_copy(k, slots.at[0:SLOT]).wait_recv()
                build(k + 1, slots_in.at[k])
                build(k + 3, slots_in.at[k])
            table_copy(c, k, source[c].at[0:own]).wait_recv()
            extract(c, k + 1, tables[c][k].reshape(rows, CHUNKS[c]))
        if AHEAD == 2 and c + 2 < count:
            send_own(c + 2)
        for k in range(2, 4):
            extract(c, k + 3, tables[c][k].reshape(rows, CHUNKS[c]))

    def slot_rows(owner, low=0, high=None):
        high = rows if high is None else high
        return pl.ds(pl.multiple_of(owner * rows + low, BLOCK), high - low)

    half = rows // 2
    pieces = [(0, 0, half), (0, half, rows), (0, half, rows), (0, 0, half)]
    pieces += [(-1, 0, half), (1, half, rows)]

    def ring_copy(c, k):
        dx, low, high = pieces[k]
        at = gathered[c].at[slot_rows(peer(dx), low, high)]
        return remote(at, at, ring_send.at[c, k], ring_recv.at[c, k], (graph, peer(ring[k % 2])))

    def pair_copy(c, k):
        at = gathered[c].at[slot_rows(peer((0, -1, 1, 2)[k]))]
        return remote(at, at, pair_send.at[c, k], pair_recv.at[c, k], (graph, peer(0, 1)))

    def blend(c):
        remote(
            staged[c], staged[c],
            halo_send.at[c], halo_recv.at[c], (graph, peer(0, 1)),
        ).wait_recv()
        for b in range(rows // BLOCK):
            chosen = [source[c][blocks_ref[b, n]] for n in range(blocks_ref.shape[1])]
            here = slice(b * BLOCK, (b + 1) * BLOCK)
            mixed = jnp.dot(
                weights[here, :], jnp.concatenate(chosen, axis=0), preferred_element_type=f32
            )
            mixed = mixed + source[c][b].astype(f32)
            mixed = (mixed * scale[here, 0:1]).astype(bf16)
            own_out[here, starts[c] : starts[c] + CHUNKS[c]] = mixed
            gathered[c][
                pl.ds(pl.multiple_of(attn * rows + b * BLOCK, BLOCK), BLOCK), :
            ] = mixed
            if (b + 1) * BLOCK == half:
                go(ring_copy(c, 0))
        go(ring_copy(c, 1))
        go(ring_copy(c, 2))
        go(ring_copy(c, 3))
        go(pair_copy(c, 0))

    def pass_on(c):
        for k in range(2):
            ring_copy(c, k).wait_recv()
            go(ring_copy(c, k + 4))
        for k in range(2):
            ring_copy(c, k + 2).wait_recv()
            go(pair_copy(c, k + 1))

    def pass_last(c):
        for k in range(4, 6):
            ring_copy(c, k).wait_recv()
        go(pair_copy(c, 3))

    last = count - 1

    def squared_sum(values):
        wide = values.astype(f32)
        wide = wide * wide
        return sum(wide[:, i : i + 128] for i in range(0, values.shape[1], 128))

    def project_first(low, high):
        def one(owner, carry):
            at = slot_rows(owner)
            parts = [gathered[c][at, :] for c in range(last)]
            total[at, :] = jnp.dot(
                jnp.concatenate(parts, axis=1), folded[0 : starts[last], :],
                preferred_element_type=f32,
            )
            squares[at, :] = sum(squared_sum(values) for values in parts)
            return carry

        lax.fori_loop(low, high, one, 0)

    def project_last(owner):
        at = slot_rows(owner)
        values = gathered[last][at, :]
        made = total[at, :] + jnp.dot(values, folded[starts[last] :, :], preferred_element_type=f32)
        squared = squares[at, :] + squared_sum(values)
        mean = jnp.sum(squared, axis=1, keepdims=True) * (1.0 / sum(CHUNKS))
        made = (made * lax.rsqrt(mean + EPSILON)).astype(bf16)
        for k in range(3):
            joined[k, pl.ds(owner * own, own)] = made[:, k * width : (k + 1) * width].reshape(
                own, BLOCK, width
            )

    def pair_wait(c):
        for k in range(4):
            pair_copy(c, k).wait_recv()

    build(0, slots.at[0:SLOT])
    for c in range(count):
        first_hop(c)
        if c == 0:
            loads[3].wait()
            for b in range(edges.shape[0]):
                here = slice(b * BLOCK, (b + 1) * BLOCK)
                degree = jnp.zeros((BLOCK, BLOCK), f32)
                for n in range(edges.shape[1]):
                    value = edges[b, n].astype(f32)
                    degree = degree + value
                    weights[here, n * BLOCK : (n + 1) * BLOCK] = value.astype(bf16)
                degree = jnp.sum(degree, axis=1, keepdims=True)
                scale[here, :] = jnp.broadcast_to(lax.rsqrt(1.0 + degree), (BLOCK, BLOCK))
            for load in loads[:3]:
                load.wait()
            for i in range(gain.shape[0]):
                here = slice(i * 128, (i + 1) * 128)
                factor = jnp.broadcast_to(gain[i : i + 1, :], (128, 128)).T
                for k in range(3):
                    raised = factor * SCORE_SCALE if k == 0 else factor
                    folded[here, k * width : (k + 1) * width] = (
                        columns[k, here, :].astype(f32) * raised
                    ).astype(bf16)
        if c >= 2:
            pass_last(c - 2)
        if c >= 1:
            blend(c - 1)
        second_hop(c)
        if c >= 1:
            pass_on(c - 1)
    blend(last)
    pass_last(last - 1)
    for c in range(last):
        pair_wait(c)
    own_store = pltpu.make_async_copy(own_out, own_hbm, feature_sem.at[0])
    own_store.start()
    project_first(0, NX)
    pass_on(last)
    project_first(NX, 2 * NX)

    def near_member(index, carry):
        project_last(peer(index + index // 2))
        return carry

    lax.fori_loop(0, 3, near_member, 0)
    pass_last(last)
    project_last(peer(2))
    for k in range(4):
        pair_copy(last, k).wait_recv()
        project_last(peer((0, -1, 1, 2)[k], 1))

    first = lax.broadcasted_iota(jnp.int32, (BLOCK, width), 1) < HEAD_DIM
    ones = jnp.ones((2 * BLOCK, width), bf16)
    keys = mask_ref.shape[0]

    def pair(block, step, kind):
        low = joined[kind, mask_ref[2 * step, block]]
        high = joined[kind, mask_ref[2 * step + 1, block]]
        return jnp.concatenate([low, high], axis=0)

    def score(block, scores):
        query = joined[0, block]
        zero = jnp.zeros_like(query)
        query = jnp.concatenate(
            [jnp.where(first, query, zero), jnp.where(first, zero, query)], axis=0
        )
        top = None
        for step in range(keys // 2):
            piece = lax.dot_general(
                query, pair(block, step, 1), (((1,), (1,)), ((), ())), preferred_element_type=f32
            )
            scores[:, 2 * step * BLOCK : (2 * step + 2) * BLOCK] = piece
            piece = jnp.maximum(piece[:, :BLOCK], piece[:, BLOCK:])
            top = piece if top is None else jnp.maximum(top, piece)
        return jnp.max(top, axis=1, keepdims=True)

    def mix(block, scores, top):
        sums = jnp.zeros((2 * BLOCK, 2 * width), f32)
        for step in range(keys // 2):
            values = jnp.concatenate([pair(block, step, 2), ones], axis=1)
            piece = scores[:, 2 * step * BLOCK : (2 * step + 2) * BLOCK]
            raised = jnp.exp2(piece - top).astype(bf16)
            sums = sums + jnp.dot(raised, values, preferred_element_type=f32)
        sums = sums[:, :width] / sums[:, width:]
        return jnp.where(first, sums[:BLOCK], sums[BLOCK:]).astype(bf16)

    def attend(index, carry):
        owner = lax.rem(attn + 1 + index, 2 * NX)
        block = owner * own
        made = []
        for low in range(0, own, 2):
            top_a = score(block + low, scores_a)
            top_b = score(block + low + 1, scores_b)
            made.append(mix(block + low, scores_a, top_a))
            made.append(mix(block + low + 1, scores_b, top_b))
        at = pl.ds(pl.multiple_of(owner * rows, rows), rows)
        mixed_out[at, :] = jnp.concatenate(made, axis=0)

        @pl.when(index < 2 * NX - 1)
        def _():
            remote(
                mixed_out.at[at], mixed_in.at[:, pl.ds(first_col, width)],
                mixed_send, mixed_recv, (graph, owner),
            ).start()

        @pl.when(index == 2 * NX - 1)
        def _():
            mixed_in[:, pl.ds(first_col, width)] = mixed_out[at, :]

        return carry

    lax.fori_loop(0, 2 * NX, attend, 0)
    returned = remote(
        mixed_out.at[0 : (2 * NX - 1) * rows], mixed_out.at[0 : (2 * NX - 1) * rows],
        mixed_send, mixed_recv, (graph, peer(0, 1)),
    )
    returned.wait_recv()
    mixed_store = pltpu.make_async_copy(mixed_in, mixed_hbm, feature_sem.at[1])
    mixed_store.start()
    returned.wait_send()
    own_store.wait()
    mixed_store.wait()
    for k in range(4):
        slot_copy(k, slots.at[0:SLOT]).wait_send()
    for c in range(count):
        for k in range(4):
            table_copy(c, k, source[c].at[0:own]).wait_send()
            pair_copy(c, k).wait_send()
        for k in range(6):
            ring_copy(c, k).wait_send()
        remote(
            staged[c], staged[c],
            halo_send.at[c], halo_recv.at[c], (graph, peer(0, 1)),
        ).wait_send()


def on_device(
    features,
    send_rows,
    send_count,
    edge_blocks,
    edge_weight,
    mask_blocks,
    norm_gain,
    query_weight,
    key_weight,
    value_weight,
    out_weight,
):
    rows, model = features.shape
    members = 2 * NX
    width = 2 * HEAD_DIM
    keys = mask_blocks.shape[2] * BLOCK
    nb = edge_blocks.shape[1]
    count = len(CHUNKS)
    own = rows // BLOCK
    sources = own + NZ * NY * SLOT // BLOCK
    arriving = (NZ * NY - 5) * SLOT
    vmem = pl.BlockSpec(memory_space=pltpu.VMEM)
    smem = pl.BlockSpec(memory_space=pltpu.SMEM)
    hbm = pl.BlockSpec(memory_space=pl.ANY)
    scratch = [pltpu.VMEM((sources, BLOCK, w), bf16) for w in CHUNKS]
    scratch += [pltpu.VMEM((4, own, BLOCK, w), bf16) for w in CHUNKS]
    scratch += [pltpu.VMEM((arriving, w), bf16) for w in CHUNKS]
    scratch += [pltpu.VMEM((members * rows, w), bf16) for w in CHUNKS]
    scratch += [
        pltpu.SemaphoreType.DMA((count,)),
        pltpu.VMEM((BLOCK, BLOCK), f32),
        pltpu.VMEM((4, SLOT, 128), f32),
        pltpu.VMEM(edge_weight.shape, jnp.int32),
        pltpu.VMEM((NZ * NY * SLOT, rows), bf16),
        pltpu.VMEM((rows, nb * BLOCK), bf16),
        pltpu.VMEM((rows, BLOCK), f32),
        pltpu.VMEM((3, model, width), bf16),
        pltpu.VMEM((model, 3 * width), bf16),
        pltpu.VMEM((members * rows, 3 * width), f32),
        pltpu.VMEM((members * rows, 128), f32),
        pltpu.VMEM((rows, model), bf16),
        pltpu.VMEM((3, members * own, BLOCK, width), bf16),
        pltpu.VMEM((2 * BLOCK, keys), f32),
        pltpu.VMEM((2 * BLOCK, keys), f32),
        pltpu.VMEM((members * rows, width), bf16),
        pltpu.VMEM((rows, model), bf16),
        pltpu.SemaphoreType.DMA((4,)),
        pltpu.SemaphoreType.DMA,
        pltpu.SemaphoreType.DMA,
        pltpu.SemaphoreType.DMA((4,)),
        pltpu.SemaphoreType.DMA((4,)),
        pltpu.SemaphoreType.DMA((count, 4)),
        pltpu.SemaphoreType.DMA((count, 4)),
        pltpu.SemaphoreType.DMA((count,)),
        pltpu.SemaphoreType.DMA((count,)),
        pltpu.SemaphoreType.DMA((count, 6)),
        pltpu.SemaphoreType.DMA((count, 6)),
        pltpu.SemaphoreType.DMA((count, 4)),
        pltpu.SemaphoreType.DMA((count, 4)),
    ]
    attended, aggregated = pl.pallas_call(
        layer_kernel,
        out_shape=(jax.ShapeDtypeStruct((rows, model), bf16),) * 2,
        in_specs=[hbm, vmem, vmem, smem, smem, vmem, hbm, hbm, hbm, hbm],
        out_specs=(hbm, hbm),
        scratch_shapes=scratch,
        compiler_params=pltpu.CompilerParams(
            collective_id=1, has_side_effects=True, vmem_limit_bytes=60 * 2**20
        ),
        name="layer",
    )(
        features.reshape(own, BLOCK, model), send_rows[0], send_count, edge_blocks,
        mask_blocks[0].T, norm_gain.reshape(-1, 128), edge_weight,
        query_weight, key_weight, value_weight,
    )
    updated = jnp.dot(attended, out_weight, preferred_element_type=f32)
    return (updated + aggregated.astype(f32)).astype(bf16)


def solution(mesh):
    placed = (
        P(("graph", "attn"), None),
        P(("graph", "attn"), None, None),
        P(("graph", "attn"), None),
        P(("graph", "attn"), None),
        P(("graph", "attn"), None, None, None),
        P("graph", None, None),
        P(),
        P(),
        P(),
        P(),
        P(),
    )
    return jax.shard_map(
        on_device, mesh=mesh, in_specs=placed, out_specs=P(("graph", "attn"), None), check_vma=False
    )
```

```python
import jax
import jax.numpy as jnp
from jax import lax
from jax.experimental import pallas as pl
from jax.experimental.pallas import tpu as pltpu
from jax.sharding import PartitionSpec as P

HEAD_DIM = 64
BLOCK = 128
EPSILON = 1e-06
SCORE_SCALE = HEAD_DIM ** (-0.5) * 1.4426950408889634
NZ = 8
NY = 4
NX = 4
SLOT = 64
CHUNKS = (512, 256, 256)
AHEAD = 1
PLUS = (0, 1)
MINUS = (2, 3)
f32 = jnp.float32
bf16 = jnp.bfloat16


def layer_kernel(
    features, send_rows, send_count, blocks_ref, mask_ref, gain, edges_hbm,
    query_hbm, key_hbm, value_hbm, mixed_hbm, own_hbm, *scratch,
):
    count = len(CHUNKS)
    starts = [sum(CHUNKS[:c]) for c in range(count)]
    scratch = list(scratch)
    source = [scratch.pop(0) for _ in range(count)]
    tables = [scratch.pop(0) for _ in range(count)]
    staged = [scratch.pop(0) for _ in range(count)]
    gathered = [scratch.pop(0) for _ in range(count)]
    (
        feature_sem, slots, slots_in, edges, picks, weights, scale, columns, folded, total, squares,
        own_out, joined, scores_a, scores_b, mixed_out, mixed_in,
        column_sem, mixed_send, mixed_recv, slot_send, slot_recv, table_send, table_recv, halo_send, halo_recv,
        ring_send, ring_recv, pair_send, pair_recv,
    ) = scratch
    own = features.shape[0]
    rows = own * BLOCK
    graph = lax.axis_index("graph")
    attn = lax.axis_index("attn")
    z, y = graph // NY, graph % NY
    x, core = attn // 2, attn % 2

    def part(dz, dy=0):
        return lax.rem(z + dz + NZ, NZ) * NY + lax.rem(y + dy, NY)

    def peer(dx, flip=0):
        return lax.rem(x + dx + NX, NX) * 2 + (core if flip == 0 else 1 - core)

    def remote(src, dst, send, recv, to):
        return pltpu.make_async_remote_copy(
            src_ref=src, dst_ref=dst, send_sem=send, recv_sem=recv,
            device_id=to, device_id_type=pl.DeviceIdType.MESH,
        )

    width = 2 * HEAD_DIM
    first_col = pl.multiple_of(attn * width, width)
    loads = [
        pltpu.make_async_copy(
            ref.at[:, pl.ds(first_col, width)], columns.at[k], column_sem.at[k]
        )
        for k, ref in enumerate((query_hbm, key_hbm, value_hbm))
    ]
    loads.append(pltpu.make_async_copy(edges_hbm, edges, column_sem.at[3]))
    feature_loads = [
        pltpu.make_async_copy(
            features.at[:, :, pl.ds(starts[c], CHUNKS[c])], source[c].at[0:own], feature_sem.at[c]
        )
        for c in range(count)
    ]
    for load in feature_loads + loads:
        load.start()
    barrier = pltpu.get_barrier_semaphore()
    near = {(0, dy) for dy in range(1, NY)}
    near |= {(dz, dy) for dz in (1, -1) for dy in range(NY)}
    for dy in PLUS:
        near |= {(2, dy), (-2, -dy % NY)}
    for dy in MINUS:
        near |= {(-2, dy), (2, -dy % NY)}
    near = sorted(near)
    greeted = [(part(dz, dy), attn) for dz, dy in near]
    greeted += [(graph, peer(1)), (graph, peer(-1)), (graph, peer(0, 1))]
    greeted += [(graph, peer(2)), (graph, peer(1, 1)), (graph, peer(-1, 1)), (graph, peer(2, 1))]
    for device in greeted:
        pl.semaphore_signal(barrier, inc=1, device_id=device, device_id_type=pl.DeviceIdType.MESH)
    slots[...] = jnp.full((BLOCK, BLOCK), -1.0, f32)
    slots[0 : NZ * NY, 0:SLOT] = send_rows[...].astype(f32)
    turned = slots[...].T
    slots[...] = jnp.zeros((BLOCK, BLOCK), f32)
    slots[0:1, 0 : NZ * NY] = send_count[...].astype(f32)
    place = lax.broadcasted_iota(jnp.int32, (BLOCK, BLOCK), 0).astype(f32)
    slots[...] = jnp.where(place < slots[0:1, :], turned, -1.0)
    pl.semaphore_wait(barrier, len(greeted))

    def go(copy):
        copy.start()

    ring = [1, -1]

    def slot_copy(k, src):
        return remote(
            src, slots_in.at[k], slot_send.at[k], slot_recv.at[k], (part(ring[k % 2]), attn)
        )

    def table_copy(c, k, src):
        return remote(
            src, tables[c].at[k], table_send.at[c, k], table_recv.at[c, k],
            (part(ring[k % 2]), attn),
        )

    def send_own(c):
        feature_loads[c].wait()
        for k in range(2):
            go(table_copy(c, k, source[c].at[0:own]))

    for k in range(2):
        go(slot_copy(k, slots.at[0:SLOT]))
    for c in range(AHEAD):
        send_own(c)

    plan = [(0, [(0, dy) for dy in range(NY)])]
    for side in (1, -1):
        plan.append((-side, [(0, dy) for dy in range(NY)]))
    for side, far in ((1, PLUS), (-1, MINUS)):
        onward = [(side, dy) for dy in range(NY)] + [(2 * side, dy) for dy in far]
        plan.append((-2 * side, onward))
    for side in (1, -1):
        plan.append((-2 * side, [(0, dy) for dy in range(NY)]))
    keeps = [int(p[1][0] == (0, 0)) for p in plan]
    pick_start = [sum(len(p[1]) for p in plan[:k]) * SLOT for k in range(len(plan))]
    stage_start = [pick_start[k] - sum(keeps[:k]) * SLOT for k in range(len(plan))]

    lane = lax.broadcasted_iota(jnp.int32, (SLOT, 128), 1)
    row_number = lax.broadcasted_iota(jnp.int32, (SLOT, rows), 1).astype(f32)

    def build(k, ref):
        known = ref[...]
        for n, (dz, dy) in enumerate(plan[k][1]):
            wanted = jnp.sum(
                jnp.where(lane == part(dz, dy), known, 0.0), axis=1, keepdims=True
            )
            picks[pick_start[k] + n * SLOT : pick_start[k] + (n + 1) * SLOT, :] = jnp.where(
                row_number == wanted, 1.0, 0.0
            ).astype(bf16)

    def halo_rows(sender):
        low = pl.multiple_of(sender % 2 * SLOT, SLOT)
        return own + sender // 2, pl.ds(low, SLOT)

    def extract(c, k, table):
        sender_dz, dests = plan[k]
        sender = part(sender_dz)
        size = len(dests) * SLOT
        found = jnp.dot(
            picks[pick_start[k] : pick_start[k] + size, :], table, preferred_element_type=f32
        ).astype(bf16)
        kept = keeps[k]
        if kept:
            source[c][(*halo_rows(sender), slice(None))] = found[0:SLOT]
        at = stage_start[k]
        staged[c][at : at + size - kept * SLOT, :] = found[kept * SLOT :]
        for n, (dz, dy) in enumerate(dests[kept:]):
            go(
                remote(
                    staged[c].at[at + n * SLOT : at + (n + 1) * SLOT],
                    source[c].at[halo_rows(sender)],
                    halo_send.at[c], halo_recv.at[c], (part(dz, dy), attn),
                )
            )

    def first_hop(c):
        if c == 0:
            extract(c, 0, source[c][0:own].reshape(rows, CHUNKS[c]))
        for k in range(2):
            if c == 0:
                slot_copy(k, slots.at[0:SLOT]).wait_recv()
                go(slot_copy(k + 2, slots_in.at[k]))
            table_copy(c, k, source[c].at[0:own]).wait_recv()
            go(table_copy(c, k + 2, tables[c].at[k]))
        if AHEAD == 1 and c + 1 < count:
            send_own(c + 1)
        if c > 0:
            extract(c, 0, source[c][0:own].reshape(rows, CHUNKS[c]))
        for k in range(2):
            if c == 0:
                build(k + 1, slots_in.at[k])
            extract(c, k + 1, tables[c][k].reshape(rows, CHUNKS[c]))

    def second_hop(c):
        for k in range(2, 4):
            if c == 0:
                slot_copy(k, slots.at[0:SLOT]).wait_recv()
                build(k + 1, slots_in.at[k])
                build(k + 3, slots_in.at[k])
            table_copy(c, k, source[c].at[0:own]).wait_recv()
            extract(c, k + 1, tables[c][k].reshape(rows, CHUNKS[c]))
        if AHEAD == 2 and c + 2 < count:
            send_own(c + 2)
        for k in range(2, 4):
            extract(c, k + 3, tables[c][k].reshape(rows, CHUNKS[c]))

    def slot_rows(owner, low=0, high=None):
        high = rows if high is None else high
        return pl.ds(pl.multiple_of(owner * rows + low, BLOCK), high - low)

    half = rows // 2
    pieces = [(0, 0, half), (0, half, rows), (0, half, rows), (0, 0, half)]
    pieces += [(-1, 0, half), (1, half, rows)]

    def ring_copy(c, k):
        dx, low, high = pieces[k]
        at = gathered[c].at[slot_rows(peer(dx), low, high)]
        return remote(at, at, ring_send.at[c, k], ring_recv.at[c, k], (graph, peer(ring[k % 2])))

    def pair_copy(c, k):
        at = gathered[c].at[slot_rows(peer((0, -1, 1, 2)[k]))]
        return remote(at, at, pair_send.at[c, k], pair_recv.at[c, k], (graph, peer(0, 1)))

    def blend(c):
        remote(
            staged[c], staged[c],
            halo_send.at[c], halo_recv.at[c], (graph, peer(0, 1)),
        ).wait_recv()
        for b in range(rows // BLOCK):
            chosen = [source[c][blocks_ref[b, n]] for n in range(blocks_ref.shape[1])]
            here = slice(b * BLOCK, (b + 1) * BLOCK)
            mixed = jnp.dot(
                weights[here, :], jnp.concatenate(chosen, axis=0), preferred_element_type=f32
            )
            mixed = mixed + source[c][b].astype(f32)
            mixed = (mixed * scale[here, 0:1]).astype(bf16)
            own_out[here, starts[c] : starts[c] + CHUNKS[c]] = mixed
            gathered[c][
                pl.ds(pl.multiple_of(attn * rows + b * BLOCK, BLOCK), BLOCK), :
            ] = mixed
            if (b + 1) * BLOCK == half:
                go(ring_copy(c, 0))
        go(ring_copy(c, 1))
        go(ring_copy(c, 2))
        go(ring_copy(c, 3))
        go(pair_copy(c, 0))

    def pass_on(c):
        for k in range(2):
            ring_copy(c, k).wait_recv()
            go(ring_copy(c, k + 4))
        for k in range(2):
            ring_copy(c, k + 2).wait_recv()
            go(pair_copy(c, k + 1))

    def pass_last(c):
        for k in range(4, 6):
            ring_copy(c, k).wait_recv()
        go(pair_copy(c, 3))

    last = count - 1

    def squared_sum(values):
        wide = values.astype(f32)
        wide = wide * wide
        return sum(wide[:, i : i + 128] for i in range(0, values.shape[1], 128))

    def project_early(c, low, high):
        def one(owner, carry):
            at = slot_rows(owner)
            values = gathered[c][at, :]
            made = jnp.dot(
                values, folded[starts[c] : starts[c] + CHUNKS[c], :], preferred_element_type=f32
            )
            squared = squared_sum(values)
            if c > 0:
                made = made + total[at, :]
                squared = squared + squares[at, :]
            total[at, :] = made
            squares[at, :] = squared
            return carry

        lax.fori_loop(low, high, one, 0)

    def project_last(owner):
        at = slot_rows(owner)
        values = gathered[last][at, :]
        made = total[at, :] + jnp.dot(values, folded[starts[last] :, :], preferred_element_type=f32)
        squared = squares[at, :] + squared_sum(values)
        mean = jnp.sum(squared, axis=1, keepdims=True) * (1.0 / sum(CHUNKS))
        made = (made * lax.rsqrt(mean + EPSILON)).astype(bf16)
        for k in range(3):
            joined[k, pl.ds(owner * own, own)] = made[:, k * width : (k + 1) * width].reshape(
                own, BLOCK, width
            )

    def pair_wait(c):
        for k in range(4):
            pair_copy(c, k).wait_recv()

    build(0, slots.at[0:SLOT])
    for c in range(count):
        first_hop(c)
        if c == 0:
            loads[3].wait()
            for b in range(edges.shape[0]):
                here = slice(b * BLOCK, (b + 1) * BLOCK)
                degree = jnp.zeros((BLOCK, BLOCK), f32)
                for n in range(edges.shape[1]):
                    value = edges[b, n].astype(f32)
                    degree = degree + value
                    weights[here, n * BLOCK : (n + 1) * BLOCK] = value.astype(bf16)
                degree = jnp.sum(degree, axis=1, keepdims=True)
                scale[here, :] = jnp.broadcast_to(lax.rsqrt(1.0 + degree), (BLOCK, BLOCK))
            for load in loads[:3]:
                load.wait()
            for i in range(gain.shape[0]):
                here = slice(i * 128, (i + 1) * 128)
                factor = jnp.broadcast_to(gain[i : i + 1, :], (128, 128)).T
                for k in range(3):
                    raised = factor * SCORE_SCALE if k == 0 else factor
                    folded[here, k * width : (k + 1) * width] = (
                        columns[k, here, :].astype(f32) * raised
                    ).astype(bf16)
        if c >= 2:
            pass_last(c - 2)
        if c >= 1:
            blend(c - 1)
        second_hop(c)
        if c >= 1:
            pass_on(c - 1)
        if c >= 2:
            pair_wait(c - 2)
            project_early(c - 2, 0, 2 * NX)
    blend(last)
    pass_last(last - 1)
    pair_wait(last - 1)
    own_store = pltpu.make_async_copy(own_out, own_hbm, feature_sem.at[0])
    own_store.start()
    project_early(last - 1, 0, NX)
    pass_on(last)
    project_early(last - 1, NX, 2 * NX)

    def near_member(index, carry):
        project_last(peer(index + index // 2))
        return carry

    lax.fori_loop(0, 3, near_member, 0)
    pass_last(last)
    project_last(peer(2))
    for k in range(4):
        pair_copy(last, k).wait_recv()
        project_last(peer((0, -1, 1, 2)[k], 1))

    first = lax.broadcasted_iota(jnp.int32, (BLOCK, width), 1) < HEAD_DIM
    ones = jnp.ones((2 * BLOCK, width), bf16)
    keys = mask_ref.shape[0]

    def pair(block, step, kind):
        low = joined[kind, mask_ref[2 * step, block]]
        high = joined[kind, mask_ref[2 * step + 1, block]]
        return jnp.concatenate([low, high], axis=0)

    def score(block, scores):
        query = joined[0, block]
        zero = jnp.zeros_like(query)
        query = jnp.concatenate(
            [jnp.where(first, query, zero), jnp.where(first, zero, query)], axis=0
        )
        top = None
        for step in range(keys // 2):
            piece = lax.dot_general(
                query, pair(block, step, 1), (((1,), (1,)), ((), ())), preferred_element_type=f32
            )
            scores[:, 2 * step * BLOCK : (2 * step + 2) * BLOCK] = piece
            piece = jnp.maximum(piece[:, :BLOCK], piece[:, BLOCK:])
            top = piece if top is None else jnp.maximum(top, piece)
        return jnp.max(top, axis=1, keepdims=True)

    def mix(block, scores, top):
        sums = jnp.zeros((2 * BLOCK, 2 * width), f32)
        for step in range(keys // 2):
            values = jnp.concatenate([pair(block, step, 2), ones], axis=1)
            piece = scores[:, 2 * step * BLOCK : (2 * step + 2) * BLOCK]
            raised = jnp.exp2(piece - top).astype(bf16)
            sums = sums + jnp.dot(raised, values, preferred_element_type=f32)
        sums = sums[:, :width] / sums[:, width:]
        return jnp.where(first, sums[:BLOCK], sums[BLOCK:]).astype(bf16)

    def attend(index, carry):
        owner = lax.rem(attn + 1 + index, 2 * NX)
        block = owner * own
        made = []
        for low in range(0, own, 2):
            top_a = score(block + low, scores_a)
            top_b = score(block + low + 1, scores_b)
            made.append(mix(block + low, scores_a, top_a))
            made.append(mix(block + low + 1, scores_b, top_b))
        at = pl.ds(pl.multiple_of(owner * rows, rows), rows)
        mixed_out[at, :] = jnp.concatenate(made, axis=0)

        @pl.when(index < 2 * NX - 1)
        def _():
            remote(
                mixed_out.at[at], mixed_in.at[:, pl.ds(first_col, width)],
                mixed_send, mixed_recv, (graph, owner),
            ).start()

        @pl.when(index == 2 * NX - 1)
        def _():
            mixed_in[:, pl.ds(first_col, width)] = mixed_out[at, :]

        return carry

    lax.fori_loop(0, 2 * NX, attend, 0)
    returned = remote(
        mixed_out.at[0 : (2 * NX - 1) * rows], mixed_out.at[0 : (2 * NX - 1) * rows],
        mixed_send, mixed_recv, (graph, peer(0, 1)),
    )
    returned.wait_recv()
    mixed_store = pltpu.make_async_copy(mixed_in, mixed_hbm, feature_sem.at[1])
    mixed_store.start()
    returned.wait_send()
    own_store.wait()
    mixed_store.wait()
    for k in range(4):
        slot_copy(k, slots.at[0:SLOT]).wait_send()
    for c in range(count):
        for k in range(4):
            table_copy(c, k, source[c].at[0:own]).wait_send()
            pair_copy(c, k).wait_send()
        for k in range(6):
            ring_copy(c, k).wait_send()
        remote(
            staged[c], staged[c],
            halo_send.at[c], halo_recv.at[c], (graph, peer(0, 1)),
        ).wait_send()


def on_device(
    features,
    send_rows,
    send_count,
    edge_blocks,
    edge_weight,
    mask_blocks,
    norm_gain,
    query_weight,
    key_weight,
    value_weight,
    out_weight,
):
    rows, model = features.shape
    members = 2 * NX
    width = 2 * HEAD_DIM
    keys = mask_blocks.shape[2] * BLOCK
    nb = edge_blocks.shape[1]
    count = len(CHUNKS)
    own = rows // BLOCK
    sources = own + NZ * NY * SLOT // BLOCK
    arriving = (NZ * NY - 5) * SLOT
    vmem = pl.BlockSpec(memory_space=pltpu.VMEM)
    smem = pl.BlockSpec(memory_space=pltpu.SMEM)
    hbm = pl.BlockSpec(memory_space=pl.ANY)
    scratch = [pltpu.VMEM((sources, BLOCK, w), bf16) for w in CHUNKS]
    scratch += [pltpu.VMEM((4, own, BLOCK, w), bf16) for w in CHUNKS]
    scratch += [pltpu.VMEM((arriving, w), bf16) for w in CHUNKS]
    scratch += [pltpu.VMEM((members * rows, w), bf16) for w in CHUNKS]
    scratch += [
        pltpu.SemaphoreType.DMA((count,)),
        pltpu.VMEM((BLOCK, BLOCK), f32),
        pltpu.VMEM((4, SLOT, 128), f32),
        pltpu.VMEM(edge_weight.shape, jnp.int32),
        pltpu.VMEM((NZ * NY * SLOT, rows), bf16),
        pltpu.VMEM((rows, nb * BLOCK), bf16),
        pltpu.VMEM((rows, BLOCK), f32),
        pltpu.VMEM((3, model, width), bf16),
        pltpu.VMEM((model, 3 * width), bf16),
        pltpu.VMEM((members * rows, 3 * width), f32),
        pltpu.VMEM((members * rows, 128), f32),
        pltpu.VMEM((rows, model), bf16),
        pltpu.VMEM((3, members * own, BLOCK, width), bf16),
        pltpu.VMEM((2 * BLOCK, keys), f32),
        pltpu.VMEM((2 * BLOCK, keys), f32),
        pltpu.VMEM((members * rows, width), bf16),
        pltpu.VMEM((rows, model), bf16),
        pltpu.SemaphoreType.DMA((4,)),
        pltpu.SemaphoreType.DMA,
        pltpu.SemaphoreType.DMA,
        pltpu.SemaphoreType.DMA((4,)),
        pltpu.SemaphoreType.DMA((4,)),
        pltpu.SemaphoreType.DMA((count, 4)),
        pltpu.SemaphoreType.DMA((count, 4)),
        pltpu.SemaphoreType.DMA((count,)),
        pltpu.SemaphoreType.DMA((count,)),
        pltpu.SemaphoreType.DMA((count, 6)),
        pltpu.SemaphoreType.DMA((count, 6)),
        pltpu.SemaphoreType.DMA((count, 4)),
        pltpu.SemaphoreType.DMA((count, 4)),
    ]
    attended, aggregated = pl.pallas_call(
        layer_kernel,
        out_shape=(jax.ShapeDtypeStruct((rows, model), bf16),) * 2,
        in_specs=[hbm, vmem, vmem, smem, smem, vmem, hbm, hbm, hbm, hbm],
        out_specs=(hbm, hbm),
        scratch_shapes=scratch,
        compiler_params=pltpu.CompilerParams(
            collective_id=1, has_side_effects=True, vmem_limit_bytes=60 * 2**20
        ),
        name="layer",
    )(
        features.reshape(own, BLOCK, model), send_rows[0], send_count, edge_blocks,
        mask_blocks[0].T, norm_gain.reshape(-1, 128), edge_weight,
        query_weight, key_weight, value_weight,
    )
    updated = jnp.dot(attended, out_weight, preferred_element_type=f32)
    return (updated + aggregated.astype(f32)).astype(bf16)


def solution(mesh):
    placed = (
        P(("graph", "attn"), None),
        P(("graph", "attn"), None, None),
        P(("graph", "attn"), None),
        P(("graph", "attn"), None),
        P(("graph", "attn"), None, None, None),
        P("graph", None, None),
        P(),
        P(),
        P(),
        P(),
        P(),
    )
    return jax.shard_map(
        on_device, mesh=mesh, in_specs=placed, out_specs=P(("graph", "attn"), None), check_vma=False
    )
```
